32 devices in a mesh: dp: 8 (over z, x), row: 2 (over y), col: 2 (over core).
Axes of the slice: x: 2, y: 2, z: 4, core: 2. Of those that a mesh axis runs over, the one named last changes fastest.
Arguments:
- features: bfloat16 [8, 8, 64, 2048], P('dp', 'row', 'col'), may hold values from -6 to 6
- cotangent: bfloat16 [8, 8, 64, 2048], P('dp', 'row', 'col'), may hold values from -6 to 6
- kernel_one: float32 [4, 512, 1152], P(('row', 'col'), 'dp'), may hold values from -0.1875 to 0.1875
- kernel_two: float32 [4, 512, 1152], P(('row', 'col'), 'dp'), may hold values from -0.1875 to 0.1875
- gain_one: float32 [4, 512], P(('row', 'col'), 'dp'), may hold values from 0.5 to 1.5
- gain_two: float32 [4, 512], P(('row', 'col'), 'dp'), may hold values from 0.5 to 1.5
Outputs:
- outputs: bfloat16 [8, 8, 64, 2048], P('dp', 'row', 'col')
- input_grad: bfloat16 [8, 8, 64, 2048], P('dp', 'row', 'col')
- kernel_grad_one: float32 [4, 512, 1152], P(('row', 'col'), 'dp')
- kernel_grad_two: float32 [4, 512, 1152], P(('row', 'col'), 'dp')
The draws below stay inside these ranges and needn't reach their ends.
All inputs are finite; a program needn't handle non-finite values.
Results may differ from the reference program's by a relative error of at most 0.028.
Values may be sent and summed in bfloat16 or wider, within the bound.
No kernel may reach another device: no remote copies, remote signals or barrier semaphores. Data moves between devices by JAX's collectives and lax.ppermute only.
A program may use at most 128 MiB of HBM per device.

```python
import math
import jax
import jax.numpy as jnp
from jax import lax

C = 2048
GROUP = 128
IMAGES = 8
HEIGHT = 8
WIDTH = 64
BLOCKS = 4


def shard_levels(key, shape, pieces, least, top_value):
    loudness = 1.0
    for position, blocks in pieces:
        draws = jax.random.uniform(jax.random.fold_in(jax.random.fold_in(key, 6), position), (blocks,), jnp.float32, least / len(pieces), top_value / len(pieces))
        loudness = loudness * jnp.repeat(jnp.exp(draws), shape[position] // blocks).reshape((-1,) + (1,) * (len(shape) - 1 - position))
    return loudness


def bell_draw(stream_key, dims, scale, most, pieces=(), kind=jnp.bfloat16):
    level = shard_levels(stream_key, dims, pieces, -0.22, 0.18) if pieces else 1.0
    drawn = jax.random.normal(stream_key, dims, jnp.float32) * scale * level
    return jnp.minimum(jnp.maximum(drawn, -most), most).astype(kind)


def setup_inputs(seed: int = 0) -> dict:
    splits = jax.random.split(jax.random.key(seed), 7)
    features = bell_draw(splits[0], (IMAGES, HEIGHT, WIDTH, C), 1.0, 6.0, ((0, 8), (1, 2), (2, 2)))
    cotangent = bell_draw(splits[1], (IMAGES, HEIGHT, WIDTH, C), 1.0, 6.0, ((0, 8), (1, 2), (2, 2)))
    kernel_one = bell_draw(splits[2], (BLOCKS, C // BLOCKS, 9 * GROUP), (9 * GROUP) ** -0.5, 0.1875, ((0, 4), (1, 8)), jnp.float32)
    kernel_two = bell_draw(splits[3], (BLOCKS, C // BLOCKS, 9 * GROUP), (9 * GROUP) ** -0.5, 0.1875, ((0, 4), (1, 8)), jnp.float32)
    gain_one = jnp.clip(1.0 + 0.1 * jax.random.normal(splits[4], (BLOCKS, C // BLOCKS), jnp.float32), 0.5, 1.5)
    gain_two = jnp.clip(1.0 + 0.1 * jax.random.normal(splits[5], (BLOCKS, C // BLOCKS), jnp.float32), 0.5, 1.5)
    return dict(features=features, cotangent=cotangent, kernel_one=kernel_one, kernel_two=kernel_two, gain_one=gain_one, gain_two=gain_two)


GAMMA = 1.7015043497085571
ALPHA = 0.2
EPS = 1e-06

def activate(value):
    return jax.nn.gelu(value, approximate=True) * GAMMA

def act_pull(value, grad):
    _, pull = jax.vjp(activate, value)
    return pull(grad)[0]

def standardize(kernel, gain):
    mean = lax.optimization_barrier(jnp.mean(kernel, axis=-1, keepdims=True))
    centered = kernel - mean
    spread = lax.optimization_barrier(jnp.mean(centered * centered, axis=-1, keepdims=True))
    return gain[..., None] * centered * lax.rsqrt(spread + EPS) / math.sqrt(kernel.shape[-1])

def conv_forward(padded, kernel, group):
    images, hp, wp, chans = padded.shape
    height, width, groups = (hp - 2, wp - 2, chans // group)
    kern = kernel.astype(jnp.float32).reshape(groups, group, 9, group)
    total = jnp.zeros((images, height, width, groups, group), jnp.float32)
    for tap in range(9):
        row_off, col_off = (tap // 3, tap % 3)
        piece = padded[:, row_off:row_off + height, col_off:col_off + width, :].astype(jnp.float32)
        piece = piece.reshape(images, height, width, groups, group)
        total = total + jnp.einsum('bhwgi,goi->bhwgo', piece, kern[:, :, tap, :], precision=lax.Precision.HIGHEST)
    return total.reshape(images, height, width, chans)

def conv_adjoint(padded, kernel, group):
    images, hp, wp, chans = padded.shape
    height, width, groups = (hp - 2, wp - 2, chans // group)
    kern = kernel.astype(jnp.float32).reshape(groups, group, 9, group)
    total = jnp.zeros((images, height, width, groups, group), jnp.float32)
    for tap in range(9):
        row_off, col_off = (tap // 3, tap % 3)
        piece = padded[:, 2 - row_off:2 - row_off + height, 2 - col_off:2 - col_off + width, :].astype(jnp.float32)
        piece = piece.reshape(images, height, width, groups, group)
        total = total + jnp.einsum('bhwgo,goi->bhwgi', piece, kern[:, :, tap, :], precision=lax.Precision.HIGHEST)
    return total.reshape(images, height, width, chans)

def kernel_terms(grad_out, padded, group):
    images, height, width, chans = grad_out.shape
    groups = chans // group
    upper = grad_out.astype(jnp.float32).reshape(images, height, width, groups, group)
    terms = []
    for tap in range(9):
        row_off, col_off = (tap // 3, tap % 3)
        piece = padded[:, row_off:row_off + height, col_off:col_off + width, :].astype(jnp.float32)
        piece = piece.reshape(images, height, width, groups, group)
        terms.append(jnp.einsum('bhwgo,bhwgi->goi', upper, piece, precision=lax.Precision.HIGHEST))
    return jnp.stack(terms, axis=2).reshape(chans, 9 * group)

def pad_map(value):
    return jnp.pad(value, ((0, 0), (1, 1), (1, 1), (0, 0)))

def reference(features, cotangent, kernel_one, kernel_two, gain_one, gain_two):
    blocks, block_rows, fan = kernel_one.shape
    chans = blocks * block_rows
    flat_one = kernel_one.reshape(chans, fan)
    flat_two = kernel_two.reshape(chans, fan)
    gains_one = gain_one.reshape(chans)
    gains_two = gain_two.reshape(chans)
    w_one = standardize(flat_one, gains_one).astype(jnp.bfloat16)
    w_two = standardize(flat_two, gains_two).astype(jnp.bfloat16)

    def one_image(carry, pair):
        image, grad_image = pair
        image = image[None]
        grad_image = grad_image[None]
        first = activate(image.astype(jnp.float32)).astype(jnp.bfloat16)
        pad_first = pad_map(first)
        hidden_pre = conv_forward(pad_first, w_one, GROUP).astype(jnp.bfloat16)
        hidden = activate(hidden_pre.astype(jnp.float32)).astype(jnp.bfloat16)
        pad_hidden = pad_map(hidden)
        result = (image.astype(jnp.float32) + ALPHA * conv_forward(pad_hidden, w_two, GROUP)).astype(jnp.bfloat16)
        upper = (ALPHA * grad_image.astype(jnp.float32)).astype(jnp.bfloat16)
        hidden_grad = conv_adjoint(pad_map(upper), w_two, GROUP)
        lower = act_pull(hidden_pre.astype(jnp.float32), hidden_grad).astype(jnp.bfloat16)
        back = conv_adjoint(pad_map(lower), w_one, GROUP)
        in_grad = (grad_image.astype(jnp.float32) + act_pull(image.astype(jnp.float32), back)).astype(jnp.bfloat16)
        sum_one = carry[0] + kernel_terms(lower, pad_first, GROUP)
        sum_two = carry[1] + kernel_terms(upper, pad_hidden, GROUP)
        return ((sum_one, sum_two), (result[0], in_grad[0]))
    start = (jnp.zeros((chans, fan), jnp.float32), jnp.zeros((chans, fan), jnp.float32))
    sums, stacked = lax.scan(one_image, start, (features, cotangent))
    _, pull_one = jax.vjp(standardize, flat_one, gains_one)
    _, pull_two = jax.vjp(standardize, flat_two, gains_two)
    grad_one = pull_one(sums[0])[0].reshape(blocks, block_rows, fan)
    grad_two = pull_two(sums[1])[0].reshape(blocks, block_rows, fan)
    return (stacked[0], stacked[1], grad_one, grad_two)
```

```python
import functools
import math

import jax
import jax.numpy as jnp
from jax import lax
from jax.experimental import pallas as pl
from jax.experimental.pallas import tpu as pltpu
from jax.sharding import Mesh, PartitionSpec as P

GAMMA = 1.7015043497085571
ALPHA = 0.2
EPS = 1e-06
ROOT = math.sqrt(2.0 / math.pi)
CUBE = 0.044715
F32 = jnp.float32
BF16 = jnp.bfloat16
VMEM_LIMIT = 48 * 1024 * 1024


def act_value(x):
    t = jnp.tanh(ROOT * (x + CUBE * (x * x * x)))
    return (0.5 * GAMMA) * x * (1.0 + t)


def act_slope(x):
    sq = x * x
    t = jnp.tanh(ROOT * (x + CUBE * (sq * x)))
    return (0.5 * GAMMA) * ((1.0 + t) + x * (1.0 - t * t) * (ROOT + (3.0 * CUBE * ROOT) * sq))


def act_both(x):
    sq = x * x
    t = jnp.tanh(ROOT * (x + CUBE * (sq * x)))
    up = 1.0 + t
    value = (0.5 * GAMMA) * x * up
    slope = (0.5 * GAMMA) * (up + x * (1.0 - t * t) * (ROOT + (3.0 * CUBE * ROOT) * sq))
    return value, slope


def params(**kw):
    return pltpu.CompilerParams(vmem_limit_bytes=VMEM_LIMIT, **kw)


def cost(flops, size):
    return pl.CostEstimate(flops=int(flops), bytes_accessed=int(size), transcendentals=0)


def column(gain_ref):
    rows = gain_ref.shape[1]
    first = lax.broadcasted_iota(jnp.int32, (rows, rows), 0)
    second = lax.broadcasted_iota(jnp.int32, (rows, rows), 1)
    spread = jnp.broadcast_to(gain_ref[...], (rows, rows))
    return jnp.sum(jnp.where(first == second, spread, 0.0), axis=1, keepdims=True)


def std_kernel(k1, k2, g1, g2, w1, w2):
    for k, g, w in ((k1, g1, w1), (k2, g2, w2)):
        fan = k.shape[1]
        kern = k[...]
        cent = kern - jnp.mean(kern, axis=1, keepdims=True)
        var = jnp.mean(cent * cent, axis=1, keepdims=True)
        scale = column(g) * lax.rsqrt(var + EPS) * (1.0 / math.sqrt(fan))
        w[...] = (cent * scale).astype(BF16)


def std_rows(k1, k2, g1, g2):
    shape = jax.ShapeDtypeStruct(k1.shape, BF16)
    return pl.pallas_call(
        std_kernel,
        out_shape=(shape, shape),
        name="std_rows",
        compiler_params=params(),
        cost_estimate=cost(1e6, 4e6),
    )(k1, k2, g1, g2)


def pull_kernel(k, g, keep, recv, out):
    fan = k.shape[1]
    kern = k[...]
    grad = keep[...].astype(F32) + recv[...].astype(F32)
    cent = kern - jnp.mean(kern, axis=1, keepdims=True)
    var = jnp.mean(cent * cent, axis=1, keepdims=True)
    inv = lax.rsqrt(var + EPS)
    scale = column(g) * inv * (1.0 / math.sqrt(fan))
    dot = jnp.mean(grad * cent, axis=1, keepdims=True)
    term = scale * (grad - cent * (inv * inv * dot))
    out[...] = term - jnp.mean(term, axis=1, keepdims=True)


def pull_rows(k, g, keep, recv):
    return pl.pallas_call(
        pull_kernel,
        out_shape=jax.ShapeDtypeStruct(k.shape, F32),
        name="pull_rows",
        compiler_params=params(),
        cost_estimate=cost(1e6, 4e6),
    )(k, g, keep, recv)


def pack_kernel(geo, f, c, out):
    cells = f.shape[0]
    group = geo["group"]
    for dst in range(geo["peers"]):
        b, block = dst // geo["blocks"], dst % geo["blocks"]
        for slot in range(geo["slots"]):
            at = (block * geo["per_block"] + slot * geo["nb"] + b) * group
            out[dst, 0, slot] = act_value(f[:, at : at + group].astype(F32)).astype(BF16)
            out[dst, 1, slot] = (ALPHA * c[:, at : at + group].astype(F32)).astype(BF16)


def pack(geo, f, c):
    cells = f.shape[0]
    return pl.pallas_call(
        functools.partial(pack_kernel, geo),
        out_shape=jax.ShapeDtypeStruct((geo["peers"], 2, geo["slots"], cells, geo["group"]), BF16),
        name="pack",
        compiler_params=params(),
        cost_estimate=cost(4e6, 4e6),
    )(f, c)


def merge_kernel(geo, f, c, recv, out, grad):
    group = geo["group"]
    for src in range(geo["peers"]):
        b, block = src // geo["blocks"], src % geo["blocks"]
        for slot in range(geo["slots"]):
            at = (block * geo["per_block"] + slot * geo["nb"] + b) * group
            x = f[:, at : at + group].astype(F32)
            out[:, at : at + group] = (x + recv[src, 0, slot].astype(F32)).astype(BF16)
            grad[:, at : at + group] = (
                c[:, at : at + group].astype(F32) + act_slope(x) * recv[src, 1, slot].astype(F32)
            ).astype(BF16)


def merge(geo, f, c, recv):
    shape = jax.ShapeDtypeStruct(f.shape, BF16)
    return pl.pallas_call(
        functools.partial(merge_kernel, geo),
        out_shape=(shape, shape),
        name="merge",
        compiler_params=params(),
        cost_estimate=cost(4e6, 6e6),
    )(f, c, recv)


def chunks(geo):
    nr, nc, rows, cols, images = (geo[k] for k in ("nr", "nc", "rows", "cols", "images"))
    for b in range(geo["nb"]):
        for i in range(images):
            runs = []
            for r in range(nr):
                for y in range(rows):
                    for c in range(nc):
                        runs.append(((b * nr + r) * nc + c, (i * rows + y) * cols))
            yield runs


def read_maps(geo, recv):
    cols = geo["cols"]
    return [
        jnp.concatenate([recv[peer, 0, 0, at : at + cols, :] for peer, at in runs], axis=0)
        for runs in chunks(geo)
    ]


def write_maps(geo, out, which, maps):
    cols = geo["cols"]
    for value, runs in zip(maps, chunks(geo)):
        for n, (peer, at) in enumerate(runs):
            out[peer, which, 0, at : at + cols, :] = value[n * cols : (n + 1) * cols, :]


def fill_patches(geo, x3, number, value):
    width, group, area = geo["width"], geo["group"], geo["area"]
    x = value.astype(F32)
    at = lax.broadcasted_iota(jnp.int32, (area, group), 0) % width
    left = jnp.where(at == 0, 0.0, pltpu.roll(x, 1, 0))
    right = jnp.where(at == width - 1, 0.0, pltpu.roll(x, area - 1, 0))
    zero = jnp.zeros((width, 3 * group), BF16)
    x3[number, 0:width, :] = zero
    x3[number, width + area : 2 * width + area, :] = zero
    rows = pl.ds(width, area)
    x3[number, rows, 0:group] = left.astype(BF16)
    x3[number, rows, group : 2 * group] = value.astype(BF16)
    x3[number, rows, 2 * group : 3 * group] = right.astype(BF16)


def conv(geo, x3, number, w):
    width, area, span = geo["width"], geo["area"], 3 * geo["group"]
    total = None
    for dy in range(3):
        part = lax.dot_general(
            x3[number, pl.ds(dy * width, area), :],
            w[:, dy * span : (dy + 1) * span],
            (((1,), (1,)), ((), ())),
            preferred_element_type=F32,
        )
        total = part if total is None else total + part
    return total


def adjoint(geo, x3, number, w):
    width, area, span, group = geo["width"], geo["area"], 3 * geo["group"], geo["group"]
    total = None
    for dy in range(3):
        taps = [8 - (3 * dy + s) for s in range(3)]
        rhs = jnp.concatenate([w[:, t * group : (t + 1) * group] for t in taps], axis=0)
        part = jnp.dot(x3[number, pl.ds(dy * width, area), :], rhs, preferred_element_type=F32)
        total = part if total is None else total + part
    return total


def terms(geo, grads, x3, out):
    width, area, span = geo["width"], geo["area"], 3 * geo["group"]
    for dy in range(3):
        total = None
        for number, grad in enumerate(grads):
            part = lax.dot_general(
                grad,
                x3[number, pl.ds(dy * width, area), :],
                (((0,), (0,)), ((), ())),
                preferred_element_type=F32,
            )
            total = part if total is None else total + part
        out[:, dy * span : (dy + 1) * span] = total


def load_weights(geo, refs, w):
    if not geo["pairs"]:
        w[...] = refs[0][0]
        return
    own, far = refs
    e = lax.axis_index("de")
    half = own.shape[1]
    mine = lax.axis_index("da") == pl.program_id(0)

    def put(n):
        w[pl.ds(pl.multiple_of(e * half, half), half), :] = own[n]
        w[pl.ds(pl.multiple_of((1 - e) * half, half), half), :] = far[n]

    pl.when(mine)(lambda: put(0))
    pl.when(jnp.logical_not(mine))(lambda: put(1))


def split_terms(geo, total, refs):
    if not geo["pairs"]:
        refs[0][0] = total[...]
        return
    keep, send = refs
    e = lax.axis_index("de")
    half = keep.shape[1]
    keep[0] = total[pl.ds(pl.multiple_of(e * half, half), half), :]
    send[0] = total[pl.ds(pl.multiple_of((1 - e) * half, half), half), :].astype(BF16)


def weight_specs(geo):
    fan, group = geo["fan"], geo["group"]
    if geo["pairs"]:
        return [pl.BlockSpec((2, group // 2, fan), lambda s: (0, 0, 0))] * 2
    return [pl.BlockSpec((1, group, fan), lambda s: (s, 0, 0))]


def term_out(geo):
    fan, group, slots = geo["fan"], geo["group"], geo["slots"]
    if geo["pairs"]:
        spec = pl.BlockSpec((1, group // 2, fan), lambda s: (s, 0, 0))
        return [spec] * 2, [
            jax.ShapeDtypeStruct((slots, group // 2, fan), F32),
            jax.ShapeDtypeStruct((slots, group // 2, fan), BF16),
        ]
    spec = pl.BlockSpec((1, group, fan), lambda s: (s, 0, 0))
    return [spec], [jax.ShapeDtypeStruct((slots, group, fan), F32)]


def recv_spec(geo, which):
    return pl.BlockSpec(
        (geo["peers"], 1, 1, geo["piece"], geo["group"]), lambda s: (0, which, s, 0, 0)
    )


def map_spec(geo):
    return pl.BlockSpec((1, geo["maps"], geo["area"], geo["group"]), lambda s: (s, 0, 0, 0))


def map_shape(geo):
    return jax.ShapeDtypeStruct((geo["slots"], geo["maps"], geo["area"], geo["group"]), BF16)


def scratch(geo, weights, patches, total):
    fan, group = geo["fan"], geo["group"]
    shapes = [pltpu.VMEM((group, fan), BF16) for _ in range(weights)]
    rows = geo["area"] + 2 * geo["width"]
    shapes += [pltpu.VMEM((geo["maps"], rows, 3 * group), BF16) for _ in range(patches)]
    return shapes + ([pltpu.VMEM((group, fan), F32)] if total else [])


def conv_flops(geo):
    return 2 * geo["slots"] * geo["maps"] * geo["area"] * geo["group"] * geo["fan"]


def first_kernel(geo, *refs):
    nw = 2 if geo["pairs"] else 1
    wrefs, (rec_a, rec_d, h_out, s_out) = refs[:nw], refs[nw : nw + 4]
    t_out, (w, x3, total) = refs[nw + 4 : -3], refs[-3:]
    load_weights(geo, wrefs, w)
    hidden = []
    for n, value in enumerate(read_maps(geo, rec_a)):
        fill_patches(geo, x3, n, value)
        z = conv(geo, x3, n, w).astype(BF16).astype(F32)
        h, slope = act_both(z)
        h = h.astype(BF16)
        h_out[0, n] = h
        s_out[0, n] = slope.astype(BF16)
        hidden.append(h)
    for n, h in enumerate(hidden):
        fill_patches(geo, x3, n, h)
    terms(geo, read_maps(geo, rec_d), x3, total)
    split_terms(geo, total, t_out)


def first(geo, weights, recv):
    specs, shapes = term_out(geo)
    return pl.pallas_call(
        functools.partial(first_kernel, geo),
        grid=(geo["slots"],),
        in_specs=weight_specs(geo) + [recv_spec(geo, 0), recv_spec(geo, 1)],
        out_specs=[map_spec(geo)] * 2 + specs,
        out_shape=[map_shape(geo)] * 2 + shapes,
        scratch_shapes=scratch(geo, 1, 1, True),
        name="first",
        compiler_params=params(),
        cost_estimate=cost(2 * conv_flops(geo), 6e6),
    )(*weights, recv, recv)


def lower_kernel(geo, *refs):
    nw = 2 if geo["pairs"] else 1
    wrefs, (rec_a, rec_d, s_in, l_out) = refs[:nw], refs[nw : nw + 4]
    t_out, (w, x3, y3, total) = refs[nw + 4 : -4], refs[-4:]
    load_weights(geo, wrefs, w)
    lows = []
    for n, value in enumerate(read_maps(geo, rec_d)):
        fill_patches(geo, x3, n, value)
        low = (adjoint(geo, x3, n, w) * s_in[0, n].astype(F32)).astype(BF16)
        l_out[0, n] = low
        lows.append(low)
    for n, value in enumerate(read_maps(geo, rec_a)):
        fill_patches(geo, y3, n, value)
    terms(geo, lows, y3, total)
    split_terms(geo, total, t_out)


def lower(geo, weights, recv, slope):
    specs, shapes = term_out(geo)
    return pl.pallas_call(
        functools.partial(lower_kernel, geo),
        grid=(geo["slots"],),
        in_specs=weight_specs(geo) + [recv_spec(geo, 0), recv_spec(geo, 1), map_spec(geo)],
        out_specs=[map_spec(geo)] + specs,
        out_shape=[map_shape(geo)] + shapes,
        scratch_shapes=scratch(geo, 1, 2, True),
        name="lower",
        compiler_params=params(),
        cost_estimate=cost(2 * conv_flops(geo), 6e6),
    )(*weights, recv, recv, slope)


def last_kernel(geo, *refs):
    nw = 2 if geo["pairs"] else 1
    one, two = refs[:nw], refs[nw : 2 * nw]
    h_in, l_in, out, w, x3 = refs[2 * nw :]
    load_weights(geo, two, w)
    maps = []
    for n in range(geo["maps"]):
        fill_patches(geo, x3, n, h_in[0, n])
        maps.append((ALPHA * conv(geo, x3, n, w)).astype(BF16))
    write_maps(geo, out, 0, maps)
    load_weights(geo, one, w)
    maps = []
    for n in range(geo["maps"]):
        fill_patches(geo, x3, n, l_in[0, n])
        maps.append(adjoint(geo, x3, n, w).astype(BF16))
    write_maps(geo, out, 1, maps)


def last(geo, one, two, hidden, low):
    return pl.pallas_call(
        functools.partial(last_kernel, geo),
        grid=(geo["slots"],),
        in_specs=weight_specs(geo) * 2 + [map_spec(geo)] * 2,
        out_specs=pl.BlockSpec(
            (geo["peers"], 2, 1, geo["piece"], geo["group"]), lambda s: (0, 0, s, 0, 0)
        ),
        out_shape=jax.ShapeDtypeStruct(
            (geo["peers"], 2, geo["slots"], geo["piece"], geo["group"]), BF16
        ),
        scratch_shapes=scratch(geo, 1, 1, False),
        name="last",
        compiler_params=params(),
        cost_estimate=cost(2 * conv_flops(geo), 6e6),
    )(*one, *two, hidden, low)


def fold_kernel(keep, recv, mine, send):
    a = lax.axis_index("da")
    mine[...] = keep[a] + recv[a].astype(F32)
    send[...] = (keep[1 - a] + recv[1 - a].astype(F32)).astype(BF16)


def fold(keep, recv):
    shape = keep.shape[1:]
    return pl.pallas_call(
        fold_kernel,
        out_shape=(jax.ShapeDtypeStruct(shape, F32), jax.ShapeDtypeStruct(shape, BF16)),
        name="fold",
        compiler_params=params(),
        cost_estimate=cost(1e6, 2e6),
    )(keep, recv)


def swap(value, axis):
    return lax.ppermute(value, axis, [(0, 1), (1, 0)])


def gather_rows(geo, rows):
    if not geo["pairs"]:
        return (lax.all_gather(rows, ("da", "de"), axis=0, tiled=True).reshape(
            geo["slots"], geo["group"], geo["fan"]),)
    both = jnp.stack([rows, swap(rows, "da")])
    return (both, swap(both, "de"))


def sum_rows(geo, parts, kern, gain):
    if not geo["pairs"]:
        flat = parts[0].reshape(geo["slots"] * geo["group"], geo["fan"])
        total = lax.psum_scatter(flat, ("da", "de"), scatter_dimension=0, tiled=True)
        return pull_rows(kern, gain, total, jnp.zeros_like(total))
    keep, send = parts
    mine, other = fold(keep, swap(send, "de"))
    return pull_rows(kern, gain, mine, swap(other, "da"))


def local(group, features, cotangent, kernel_one, kernel_two, gain_one, gain_two):
    images, rows, cols, chans = features.shape
    fan = kernel_one.shape[2]
    nr, nc = lax.axis_size("row"), lax.axis_size("col")
    na, nb, ne = lax.axis_size("da"), lax.axis_size("db"), lax.axis_size("de")
    blocks = nr * nc
    geo = dict(
        group=group, fan=fan, nr=nr, nc=nc, nb=nb, blocks=blocks, slots=na,
        per_block=chans // blocks // group, peers=nb * blocks, images=images,
        rows=rows, cols=cols, piece=images * rows * cols, width=nc * cols,
        area=nr * rows * nc * cols, maps=nb * images, pairs=na == 2 and ne == 2,
    )
    flat = (images * rows * cols, chans)
    f, c = features.reshape(flat), cotangent.reshape(flat)
    k1, k2 = kernel_one.reshape(-1, fan), kernel_two.reshape(-1, fan)
    w1, w2 = std_rows(k1, k2, gain_one, gain_two)
    one = gather_rows(geo, w1)
    two = gather_rows(geo, w2)
    peers = ("db", "row", "col")
    recv = lax.all_to_all(pack(geo, f, c), peers, 0, 0, tiled=True)
    hidden, slope, *terms_two = first(geo, one, recv)
    low, *terms_one = lower(geo, two, recv, slope)
    sent = last(geo, one, two, hidden, low)
    back = lax.all_to_all(sent, peers, 0, 0, tiled=True)
    outputs, input_grad = merge(geo, f, c, back)
    grad_one = sum_rows(geo, terms_one, k1, gain_one)
    grad_two = sum_rows(geo, terms_two, k2, gain_two)
    return (
        outputs.reshape(features.shape),
        input_grad.reshape(features.shape),
        grad_one.reshape(kernel_one.shape),
        grad_two.reshape(kernel_two.shape),
    )


def solution(mesh):
    names = ("da", "db", "de", "row", "col")
    nr, nc, dp = mesh.shape["row"], mesh.shape["col"], mesh.shape["dp"]

    def run(features, cotangent, kernel_one, kernel_two, gain_one, gain_two):
        group = kernel_one.shape[2] // 9
        per_block = kernel_one.shape[1] // group
        na = 2 if per_block % 2 == 0 else 1
        nb = per_block // na
        fine = Mesh(mesh.devices.reshape(na, nb, dp // per_block, nr, nc), names)
        dps = ("da", "db", "de")
        cells = P(dps, "row", "col", None)
        rows = P(("row", "col"), dps, None)
        gains = P(("row", "col"), dps)
        return jax.shard_map(
            functools.partial(local, group),
            mesh=fine,
            in_specs=(cells, cells, rows, rows, gains, gains),
            out_specs=(cells, cells, rows, rows),
            check_vma=False,
        )(features, cotangent, kernel_one, kernel_two, gain_one, gain_two)

    return run
```

```python
import functools
import math

import jax
import jax.numpy as jnp
from jax import lax
from jax.experimental import pallas as pl
from jax.experimental.pallas import tpu as pltpu
from jax.sharding import Mesh, PartitionSpec as P

GAMMA = 1.7015043497085571
ALPHA = 0.2
EPS = 1e-06
ROOT = math.sqrt(2.0 / math.pi)
CUBE = 0.044715
F32 = jnp.float32
BF16 = jnp.bfloat16
VMEM_LIMIT = 24 * 1024 * 1024
SMALL = 1
RELAY = 20_000_000_000
FIRST = 3_000_000_000
SECOND = LOWER = RELAY
PULL = MERGE = SMALL


def act_value(x):
    t = jnp.tanh(ROOT * (x + CUBE * (x * x * x)))
    return (0.5 * GAMMA) * x * (1.0 + t)


def act_slope(x):
    sq = x * x
    t = jnp.tanh(ROOT * (x + CUBE * (sq * x)))
    return (0.5 * GAMMA) * ((1.0 + t) + x * (1.0 - t * t) * (ROOT + (3.0 * CUBE * ROOT) * sq))


def act_both(x):
    sq = x * x
    t = jnp.tanh(ROOT * (x + CUBE * (sq * x)))
    up = 1.0 + t
    value = (0.5 * GAMMA) * x * up
    slope = (0.5 * GAMMA) * (up + x * (1.0 - t * t) * (ROOT + (3.0 * CUBE * ROOT) * sq))
    return value, slope


def params(**kw):
    return pltpu.CompilerParams(vmem_limit_bytes=VMEM_LIMIT, **kw)


def pin(x):
    return pltpu.with_memory_space_constraint(x, pltpu.HBM)


def cost(flops):
    return pl.CostEstimate(flops=flops, bytes_accessed=1, transcendentals=0)


def column(gain_ref):
    rows = gain_ref.shape[1]
    first = lax.broadcasted_iota(jnp.int32, (rows, rows), 0)
    second = lax.broadcasted_iota(jnp.int32, (rows, rows), 1)
    spread = jnp.broadcast_to(gain_ref[...], (rows, rows))
    return jnp.sum(jnp.where(first == second, spread, 0.0), axis=1, keepdims=True)


def std_into(k, g, w):
    fan = k.shape[1]
    kern = k[...]
    cent = kern - jnp.mean(kern, axis=1, keepdims=True)
    var = jnp.mean(cent * cent, axis=1, keepdims=True)
    scale = column(g) * lax.rsqrt(var + EPS) * (1.0 / math.sqrt(fan))
    w[...] = (cent * scale).astype(BF16)


def pull_kernel(k, g, keep, near, over, out):
    fan = k.shape[1]
    kern = k[...]
    grad = keep[...] + near[...].astype(F32) + over[...].astype(F32)
    cent = kern - jnp.mean(kern, axis=1, keepdims=True)
    var = jnp.mean(cent * cent, axis=1, keepdims=True)
    inv = lax.rsqrt(var + EPS)
    scale = column(g) * inv * (1.0 / math.sqrt(fan))
    dot = jnp.mean(grad * cent, axis=1, keepdims=True)
    term = scale * (grad - cent * (inv * inv * dot))
    out[...] = term - jnp.mean(term, axis=1, keepdims=True)


def pull_rows(k, g, sums, flops):
    return pl.pallas_call(
        pull_kernel,
        out_shape=jax.ShapeDtypeStruct(k.shape, F32),
        name="pull_rows",
        compiler_params=params(),
        cost_estimate=cost(flops),
    )(k, g, *sums)


def prep_kernel(geo, k1, k2, g1, g2, f, c, w1, w2, out, k1_in, k2_in, g1_in, g2_in, f_in, c_in, sems):
    group = geo["group"]
    span = geo["per_block"] * group
    moves = [
        pltpu.make_async_copy(src, dst, sems.at[n])
        for n, (src, dst) in enumerate(((k1, k1_in), (g1, g1_in), (k2, k2_in), (g2, g2_in)))
    ]
    for n in range(geo["blocks"]):
        cut = pl.ds(n * span, span)
        for src, dst in ((f, f_in), (c, c_in)):
            moves.append(pltpu.make_async_copy(src.at[:, cut], dst.at[:, cut], sems.at[len(moves)]))
    for move in moves:
        move.start()
    for n, (k, g, w) in enumerate(((k1_in, g1_in, w1), (k2_in, g2_in, w2))):
        moves[2 * n].wait()
        moves[2 * n + 1].wait()
        std_into(k, g, w)
    for block in range(geo["blocks"]):
        moves[4 + 2 * block].wait()
        moves[5 + 2 * block].wait()
        for b in range(geo["nb"]):
            dst = b * geo["blocks"] + block
            for slot in range(geo["slots"]):
                at = (block * geo["per_block"] + slot * geo["nb"] + b) * group
                out[dst, 0, slot] = act_value(f_in[:, at : at + group].astype(F32)).astype(BF16)
                out[dst, 1, slot] = (ALPHA * c_in[:, at : at + group].astype(F32)).astype(BF16)


def prep(geo, k1, k2, g1, g2, f, c):
    cells = f.shape[0]
    args = (k1, k2, g1, g2, f, c)
    return pl.pallas_call(
        functools.partial(prep_kernel, geo),
        in_specs=[pl.BlockSpec(memory_space=pl.ANY)] * 6,
        out_shape=[jax.ShapeDtypeStruct(k1.shape, BF16)] * 2
        + [jax.ShapeDtypeStruct((geo["peers"], 2, geo["slots"], cells, geo["group"]), BF16)],
        scratch_shapes=[pltpu.VMEM(x.shape, x.dtype) for x in args]
        + [pltpu.SemaphoreType.DMA((4 + 2 * geo["blocks"],))],
        name="prep",
        compiler_params=params(),
        cost_estimate=cost(SMALL),
    )(*[pin(x) for x in args])


def merge_kernel(geo, f, c, recv, out, grad):
    group = geo["group"]
    for src in range(geo["peers"]):
        b, block = src // geo["blocks"], src % geo["blocks"]
        for slot in range(geo["slots"]):
            at = (block * geo["per_block"] + slot * geo["nb"] + b) * group
            x = f[:, at : at + group].astype(F32)
            out[:, at : at + group] = (x + recv[src, 0, slot].astype(F32)).astype(BF16)
            grad[:, at : at + group] = (
                c[:, at : at + group].astype(F32) + act_slope(x) * recv[src, 1, slot].astype(F32)
            ).astype(BF16)


def merge(geo, f, c, recv):
    shape = jax.ShapeDtypeStruct(f.shape, BF16)
    return pl.pallas_call(
        functools.partial(merge_kernel, geo),
        out_shape=(shape, shape),
        name="merge",
        compiler_params=params(),
        cost_estimate=cost(MERGE),
    )(f, c, recv)


def chunks(geo):
    nr, nc, rows, cols, images = (geo[k] for k in ("nr", "nc", "rows", "cols", "images"))
    for b in range(geo["nb"]):
        for i in range(images):
            runs = []
            for r in range(nr):
                for y in range(rows):
                    for c in range(nc):
                        runs.append(((b * nr + r) * nc + c, (i * rows + y) * cols))
            yield runs


def read_maps(geo, recv):
    cols = geo["cols"]
    return [
        jnp.concatenate([recv[peer, 0, 0, at : at + cols, :] for peer, at in runs], axis=0)
        for runs in chunks(geo)
    ]


def write_maps(geo, out, which, maps):
    cols = geo["cols"]
    for value, runs in zip(maps, chunks(geo)):
        for n, (peer, at) in enumerate(runs):
            out[peer, which, 0, at : at + cols, :] = value[n * cols : (n + 1) * cols, :]


def fill_patches(geo, x3, number, value):
    width, group, area = geo["width"], geo["group"], geo["area"]
    x = value.astype(F32)
    at = lax.broadcasted_iota(jnp.int32, (area, group), 0) % width
    left = jnp.where(at == 0, 0.0, pltpu.roll(x, 1, 0))
    right = jnp.where(at == width - 1, 0.0, pltpu.roll(x, area - 1, 0))
    zero = jnp.zeros((width, 3 * group), BF16)
    x3[number, 0:width, :] = zero
    x3[number, width + area : 2 * width + area, :] = zero
    rows = pl.ds(width, area)
    x3[number, rows, 0:group] = left.astype(BF16)
    x3[number, rows, group : 2 * group] = value.astype(BF16)
    x3[number, rows, 2 * group : 3 * group] = right.astype(BF16)


def conv(geo, x3, number, w):
    width, area, span = geo["width"], geo["area"], 3 * geo["group"]
    total = None
    for dy in range(3):
        part = lax.dot_general(
            x3[number, pl.ds(dy * width, area), :],
            w[:, dy * span : (dy + 1) * span],
            (((1,), (1,)), ((), ())),
            preferred_element_type=F32,
        )
        total = part if total is None else total + part
    return total


def adjoint(geo, x3, number, w):
    width, area, span, group = geo["width"], geo["area"], 3 * geo["group"], geo["group"]
    total = None
    for dy in range(3):
        taps = [8 - (3 * dy + s) for s in range(3)]
        rhs = jnp.concatenate([w[:, t * group : (t + 1) * group] for t in taps], axis=0)
        part = jnp.dot(x3[number, pl.ds(dy * width, area), :], rhs, preferred_element_type=F32)
        total = part if total is None else total + part
    return total


def terms(geo, grads, x3, out):
    width, area, span = geo["width"], geo["area"], 3 * geo["group"]
    for dy in range(3):
        total = None
        for number, grad in enumerate(grads):
            part = lax.dot_general(
                grad,
                x3[number, pl.ds(dy * width, area), :],
                (((0,), (0,)), ((), ())),
                preferred_element_type=F32,
            )
            total = part if total is None else total + part
        out[:, dy * span : (dy + 1) * span] = total


def load_weights(geo, refs, w):
    if not geo["pairs"]:
        w[...] = refs[0][0]
        return
    own, far = refs
    e = lax.axis_index("de")
    half = own.shape[1]
    mine = lax.axis_index("da") == pl.program_id(0)

    def put(n):
        w[pl.ds(pl.multiple_of(e * half, half), half), :] = own[n]
        w[pl.ds(pl.multiple_of((1 - e) * half, half), half), :] = far[n]

    pl.when(mine)(lambda: put(0))
    pl.when(jnp.logical_not(mine))(lambda: put(1))


def split_terms(geo, total, refs):
    if not geo["pairs"]:
        refs[0][0] = total[...]
        return
    keep_near, keep_far, send_near, send_far = refs
    e = lax.axis_index("de")
    half = keep_near.shape[0]
    mine = lax.axis_index("da") == pl.program_id(0)

    def put(keep, send):
        keep[...] = total[pl.ds(pl.multiple_of(e * half, half), half), :]
        send[...] = total[pl.ds(pl.multiple_of((1 - e) * half, half), half), :].astype(BF16)

    pl.when(mine)(lambda: put(keep_near, send_near))
    pl.when(jnp.logical_not(mine))(lambda: put(keep_far, send_far))


def weight_specs(geo):
    fan, group = geo["fan"], geo["group"]
    if geo["pairs"]:
        return [pl.BlockSpec((2, group // 2, fan), lambda s: (0, 0, 0))] * 2
    return [pl.BlockSpec((1, group, fan), lambda s: (s, 0, 0))]


def term_out(geo):
    fan, group, slots = geo["fan"], geo["group"], geo["slots"]
    if geo["pairs"]:
        shape = (group // 2, fan)
        return [pl.BlockSpec(shape, lambda s: (0, 0))] * 4, [
            jax.ShapeDtypeStruct(shape, t) for t in (F32, F32, BF16, BF16)]
    spec = pl.BlockSpec((1, group, fan), lambda s: (s, 0, 0))
    return [spec], [jax.ShapeDtypeStruct((slots, group, fan), F32)]


def recv_spec(geo, which):
    dims = (geo["peers"], 1, 1, geo["piece"], geo["group"])
    return pl.BlockSpec(dims, lambda s: (0, which, s, 0, 0))


def send_spec(geo):
    dims = (geo["peers"], 2, 1, geo["piece"], geo["group"])
    return pl.BlockSpec(dims, lambda s: (0, 0, s, 0, 0))


def send_shape(geo):
    return jax.ShapeDtypeStruct(
        (geo["peers"], 2, geo["slots"], geo["piece"], geo["group"]), BF16)


def map_spec(geo):
    return pl.BlockSpec((1, geo["maps"], geo["area"], geo["group"]), lambda s: (s, 0, 0, 0))


def map_shape(geo):
    return jax.ShapeDtypeStruct((geo["slots"], geo["maps"], geo["area"], geo["group"]), BF16)


def scratch(geo, weights, patches, total):
    fan, group = geo["fan"], geo["group"]
    shapes = [pltpu.VMEM((group, fan), BF16) for _ in range(weights)]
    rows = geo["area"] + 2 * geo["width"]
    shapes += [pltpu.VMEM((geo["maps"], rows, 3 * group), BF16) for _ in range(patches)]
    return shapes + ([pltpu.VMEM((group, fan), F32)] if total else [])


def conv_flops(geo):
    return 2 * geo["slots"] * geo["maps"] * geo["area"] * geo["group"] * geo["fan"]


def call(geo, body, name, args, in_specs, out_specs, out_shape, scratch_shapes, flops):
    return pl.pallas_call(
        functools.partial(body, geo),
        grid=(geo["slots"],),
        in_specs=in_specs,
        out_specs=out_specs,
        out_shape=out_shape,
        scratch_shapes=scratch_shapes,
        name=name,
        compiler_params=params(),
        cost_estimate=cost(flops),
    )(*args)


def first_kernel(geo, *refs):
    nw = 2 if geo["pairs"] else 1
    rec_a, rec_d, h_out, s_out = refs[nw : nw + 4]
    t_out, (w, x3, total) = refs[nw + 4 : -3], refs[-3:]
    load_weights(geo, refs[:nw], w)
    hidden = []
    for n, value in enumerate(read_maps(geo, rec_a)):
        fill_patches(geo, x3, n, value)
        z = conv(geo, x3, n, w).astype(BF16).astype(F32)
        h, slope = act_both(z)
        hidden.append(h.astype(BF16))
        h_out[0, n] = hidden[n]
        s_out[0, n] = slope.astype(BF16)
    for n, h in enumerate(hidden):
        fill_patches(geo, x3, n, h)
    terms(geo, read_maps(geo, rec_d), x3, total)
    split_terms(geo, total, t_out)


def first(geo, one, recv):
    specs, shapes = term_out(geo)
    return call(
        geo, first_kernel, "first", (*one, recv, recv),
        weight_specs(geo) + [recv_spec(geo, 0), recv_spec(geo, 1)],
        [map_spec(geo)] * 2 + specs, [map_shape(geo)] * 2 + shapes,
        scratch(geo, 1, 1, True), FIRST)


def second_kernel(geo, *refs):
    nw = 2 if geo["pairs"] else 1
    one, two = refs[:nw], refs[nw : 2 * nw]
    rec_d, h_in, s_in, l_out, out, w1, w2, x3 = refs[2 * nw :]
    load_weights(geo, two, w2)
    maps = []
    for n in range(geo["maps"]):
        fill_patches(geo, x3, n, h_in[0, n])
        maps.append((ALPHA * conv(geo, x3, n, w2)).astype(BF16))
    write_maps(geo, out, 0, maps)
    load_weights(geo, one, w1)
    maps = []
    for n, value in enumerate(read_maps(geo, rec_d)):
        fill_patches(geo, x3, n, value)
        low = (adjoint(geo, x3, n, w2) * s_in[0, n].astype(F32)).astype(BF16)
        l_out[0, n] = low
        fill_patches(geo, x3, n, low)
        maps.append(adjoint(geo, x3, n, w1).astype(BF16))
    write_maps(geo, out, 1, maps)


def second(geo, one, two, recv, hidden, slope):
    return call(
        geo, second_kernel, "second", (*one, *two, recv, hidden, slope),
        weight_specs(geo) * 2 + [recv_spec(geo, 1)] + [map_spec(geo)] * 2,
        [map_spec(geo), send_spec(geo)], [map_shape(geo), send_shape(geo)],
        scratch(geo, 2, 1, False), SECOND)


def lower_kernel(geo, rec_a, l_in, *refs):
    t_out, (x3, total) = refs[:-2], refs[-2:]
    for n, value in enumerate(read_maps(geo, rec_a)):
        fill_patches(geo, x3, n, value)
    terms(geo, [l_in[0, n] for n in range(geo["maps"])], x3, total)
    split_terms(geo, total, t_out)


def lower(geo, recv, low):
    specs, shapes = term_out(geo)
    return call(
        geo, lower_kernel, "lower", (recv, low),
        [recv_spec(geo, 0), map_spec(geo)], specs, shapes, scratch(geo, 0, 1, True), LOWER)


def fold_kernel(keep, recv, send):
    send[...] = (keep[...] + recv[...].astype(F32)).astype(BF16)


def fold(keep, recv):
    return pl.pallas_call(
        fold_kernel,
        out_shape=jax.ShapeDtypeStruct(keep.shape, BF16),
        name="fold",
        compiler_params=params(),
        cost_estimate=cost(SMALL),
    )(keep, recv)


def swap(value, axis):
    return lax.ppermute(value, axis, [(0, 1), (1, 0)])


def relay_kernel(rows, over, out):
    out[0] = rows[...]
    out[1] = over[...]


def relay(rows, over):
    return pl.pallas_call(
        relay_kernel,
        out_shape=jax.ShapeDtypeStruct((2,) + rows.shape, rows.dtype),
        name="relay",
        compiler_params=params(),
        cost_estimate=cost(RELAY),
    )(rows, over)


def gather_rows(geo, one, two):
    if not geo["pairs"]:
        full = [lax.all_gather(w, ("da", "de"), axis=0, tiled=True) for w in (one, two)]
        return [(w.reshape(geo["slots"], geo["group"], geo["fan"]),) for w in full]
    over = swap(one, "da")
    two, over = lax.optimization_barrier((two, over))
    one = relay(one, over)
    two = relay(two, swap(two, "da"))
    return (one, swap(one, "de")), (two, swap(two, "de"))


def local(group, features, cotangent, kernel_one, kernel_two, gain_one, gain_two):
    images, rows, cols, chans = features.shape
    fan = kernel_one.shape[2]
    nr, nc = lax.axis_size("row"), lax.axis_size("col")
    na, nb, ne = lax.axis_size("da"), lax.axis_size("db"), lax.axis_size("de")
    blocks = nr * nc
    geo = dict(
        group=group, fan=fan, nr=nr, nc=nc, nb=nb, blocks=blocks, slots=na,
        per_block=chans // blocks // group, peers=nb * blocks, images=images,
        rows=rows, cols=cols, piece=images * rows * cols, width=nc * cols,
        area=nr * rows * nc * cols, maps=nb * images, pairs=na == 2 and ne == 2,
    )
    flat = (images * rows * cols, chans)
    f, c = features.reshape(flat), cotangent.reshape(flat)
    k1, k2 = kernel_one.reshape(-1, fan), kernel_two.reshape(-1, fan)
    w1, w2, pieces = prep(geo, k1, k2, gain_one, gain_two, f, c)

    def exchange(x):
        return lax.all_to_all(x, ("db", "row", "col"), 0, 0, tiled=True)

    recv = exchange(pieces)
    one, two = gather_rows(geo, w1, w2)
    hidden, slope, *parts_two = first(geo, one, recv)
    if geo["pairs"]:
        keep2, far2, send2, away2 = parts_two
        low, out = second(geo, one, two, recv, hidden, slope)
        far2 = fold(far2, swap(away2, "de"))
        out, far2 = lax.optimization_barrier((out, far2))
        back = exchange(out)
        keep1, far1, send1, away1 = lower(geo, recv, low)
        far1 = fold(far1, swap(away1, "de"))
        grad_two = pull_rows(k2, gain_two, (keep2, swap(send2, "de"), swap(far2, "da")), PULL)
        grad_one = pull_rows(k1, gain_one, (keep1, swap(send1, "de"), swap(far1, "da")), SMALL)
    else:
        low, out = second(geo, one, two, recv, hidden, slope)
        back = exchange(out)
        parts_one = lower(geo, recv, low)
        flat = jnp.stack([x[0].reshape(geo["slots"] * group, fan) for x in (parts_one, parts_two)])
        sums = lax.psum_scatter(flat, ("da", "de"), scatter_dimension=1, tiled=True)
        none = jnp.zeros(k1.shape, BF16)
        grad_one = pull_rows(k1, gain_one, (sums[0], none, none), SMALL)
        grad_two = pull_rows(k2, gain_two, (sums[1], none, none), SMALL)
    outputs, input_grad = merge(geo, f, c, back)
    return (
        outputs.reshape(features.shape),
        input_grad.reshape(features.shape),
        grad_one.reshape(kernel_one.shape),
        grad_two.reshape(kernel_two.shape),
    )


def solution(mesh):
    names = ("da", "db", "de", "row", "col")
    nr, nc, dp = mesh.shape["row"], mesh.shape["col"], mesh.shape["dp"]

    def run(features, cotangent, kernel_one, kernel_two, gain_one, gain_two):
        group = kernel_one.shape[2] // 9
        per_block = kernel_one.shape[1] // group
        na = 2 if per_block % 2 == 0 else 1
        nb = per_block // na
        fine = Mesh(mesh.devices.reshape(na, nb, dp // per_block, nr, nc), names)
        dps = ("da", "db", "de")
        cells = P(dps, "row", "col", None)
        rows = P(("row", "col"), dps, None)
        gains = P(("row", "col"), dps)
        return jax.shard_map(
            functools.partial(local, group),
            mesh=fine,
            in_specs=(cells, cells, rows, rows, gains, gains),
            out_specs=(cells, cells, rows, rows),
            check_vma=False,
        )(features, cotangent, kernel_one, kernel_two, gain_one, gain_two)

    return run
```

```python
import functools
import math

import jax
import jax.numpy as jnp
from jax import lax
from jax.experimental import pallas as pl
from jax.experimental.pallas import tpu as pltpu
from jax.sharding import Mesh, PartitionSpec as P

GAMMA = 1.7015043497085571
ALPHA = 0.2
EPS = 1e-06
ROOT = math.sqrt(2.0 / math.pi)
CUBE = 0.044715
F32 = jnp.float32
BF16 = jnp.bfloat16
VMEM_LIMIT = 24 * 1024 * 1024
SMALL = 1
RELAY = 20_000_000_000
FIRST = 3_000_000_000
LOWER = RELAY
SECOND = FOLD = RELAY
PULL = MERGE = SMALL
STRIP = 4


def act_value(x):
    t = jnp.tanh(ROOT * (x + CUBE * (x * x * x)))
    return (0.5 * GAMMA) * x * (1.0 + t)


def act_slope(x):
    sq = x * x
    t = jnp.tanh(ROOT * (x + CUBE * (sq * x)))
    return (0.5 * GAMMA) * ((1.0 + t) + x * (1.0 - t * t) * (ROOT + (3.0 * CUBE * ROOT) * sq))


def act_both(x):
    sq = x * x
    t = jnp.tanh(ROOT * (x + CUBE * (sq * x)))
    up = 1.0 + t
    value = (0.5 * GAMMA) * x * up
    slope = (0.5 * GAMMA) * (up + x * (1.0 - t * t) * (ROOT + (3.0 * CUBE * ROOT) * sq))
    return value, slope


def params(**kw):
    return pltpu.CompilerParams(vmem_limit_bytes=VMEM_LIMIT, **kw)


def pin(x):
    return pltpu.with_memory_space_constraint(x, pltpu.HBM)


def cost(flops):
    return pl.CostEstimate(flops=flops, bytes_accessed=1, transcendentals=0)


def column(gain_ref):
    rows = gain_ref.shape[1]
    first = lax.broadcasted_iota(jnp.int32, (rows, rows), 0)
    second = lax.broadcasted_iota(jnp.int32, (rows, rows), 1)
    spread = jnp.broadcast_to(gain_ref[...], (rows, rows))
    return jnp.sum(jnp.where(first == second, spread, 0.0), axis=1, keepdims=True)


def std_into(k, g, w):
    fan = k.shape[1]
    kern = k[...]
    cent = kern - jnp.mean(kern, axis=1, keepdims=True)
    var = jnp.mean(cent * cent, axis=1, keepdims=True)
    scale = column(g) * lax.rsqrt(var + EPS) * (1.0 / math.sqrt(fan))
    w[...] = (cent * scale).astype(BF16)


def pull_kernel(k, g, *refs):
    out = refs[-1]
    fan = k.shape[1]
    kern = k[...]
    grad = sum(ref[...].astype(F32) for ref in refs[:-1])
    cent = kern - jnp.mean(kern, axis=1, keepdims=True)
    var = jnp.mean(cent * cent, axis=1, keepdims=True)
    inv = lax.rsqrt(var + EPS)
    scale = column(g) * inv * (1.0 / math.sqrt(fan))
    dot = jnp.mean(grad * cent, axis=1, keepdims=True)
    term = scale * (grad - cent * (inv * inv * dot))
    out[...] = term - jnp.mean(term, axis=1, keepdims=True)


def pull_rows(k, g, sums, flops):
    return pl.pallas_call(
        pull_kernel,
        out_shape=jax.ShapeDtypeStruct(k.shape, F32),
        name="pull_rows",
        compiler_params=params(),
        cost_estimate=cost(flops),
    )(k, g, *sums)


def prep_kernel(geo, k1, k2, g1, g2, f, c, w1, w2, out, *scratch):
    k1_in, k2_in, g1_in, g2_in, f_in, c_in, stage, sems, sent = scratch
    group, blocks = geo["group"], geo["blocks"]
    span = geo["per_block"] * group

    def bring(src, dst):
        move = pltpu.make_async_copy(src, dst, sems.at[len(moves)])
        moves.append(move)
        move.start()
        return move

    moves, cells = [], []
    for n in range(blocks):
        cut = pl.ds(n * span, span)
        cells.append((bring(f.at[:, cut], f_in.at[:, cut]), bring(c.at[:, cut], c_in.at[:, cut])))
        if n == 0:
            rows = [bring(*pair) for pair in ((k1, k1_in), (g1, g1_in), (k2, k2_in), (g2, g2_in))]
    leaves = []
    for block in range(blocks):
        for move in cells[block]:
            move.wait()
        for b in range(geo["nb"]):
            dst = b * blocks + block
            for slot in range(geo["slots"]):
                at = (block * geo["per_block"] + slot * geo["nb"] + b) * group
                stage[dst, 0, slot] = act_value(f_in[:, at : at + group].astype(F32)).astype(BF16)
                stage[dst, 1, slot] = (ALPHA * c_in[:, at : at + group].astype(F32)).astype(BF16)
            leaves.append(pltpu.make_async_copy(stage.at[dst], out.at[dst], sent.at[dst]))
            leaves[-1].start()
        if block == 0:
            for move in rows[:2]:
                move.wait()
            std_into(k1_in, g1_in, w1)
            for move in rows[2:]:
                move.wait()
            std_into(k2_in, g2_in, w2)
    for move in leaves:
        move.wait()


def prep(geo, k1, k2, g1, g2, f, c):
    args = (k1, k2, g1, g2, f, c)
    dims = (geo["peers"], 2, geo["slots"], f.shape[0], geo["group"])
    vmem, hbm = (pl.BlockSpec(memory_space=m) for m in (pltpu.VMEM, pl.ANY))
    return pl.pallas_call(
        functools.partial(prep_kernel, geo),
        in_specs=[hbm] * 6,
        out_specs=[vmem, vmem, hbm],
        out_shape=[jax.ShapeDtypeStruct(k1.shape, BF16)] * 2 + [jax.ShapeDtypeStruct(dims, BF16)],
        scratch_shapes=[pltpu.VMEM(x.shape, x.dtype) for x in args] + [
            pltpu.VMEM(dims, BF16),
            pltpu.SemaphoreType.DMA((4 + 2 * geo["blocks"],)),
            pltpu.SemaphoreType.DMA((geo["peers"],))],
        name="prep",
        compiler_params=params(),
        cost_estimate=cost(SMALL),
    )(*[pin(x) for x in args])


def merge_kernel(geo, f, c, recv, out, grad, out_in, grad_in, sems):
    group, blocks = geo["group"], geo["blocks"]
    span = geo["per_block"] * group
    moves = []
    for block in range(blocks):
        for b in range(geo["nb"]):
            src = b * blocks + block
            for slot in range(geo["slots"]):
                at = (block * geo["per_block"] + slot * geo["nb"] + b) * group
                x = f[:, at : at + group].astype(F32)
                out_in[:, at : at + group] = (x + recv[src, 0, slot].astype(F32)).astype(BF16)
                grad_in[:, at : at + group] = (
                    c[:, at : at + group].astype(F32)
                    + act_slope(x) * recv[src, 1, slot].astype(F32)
                ).astype(BF16)
        cut = pl.ds(block * span, span)
        for n, (src, dst) in enumerate(((out_in, out), (grad_in, grad))):
            moves.append(pltpu.make_async_copy(
                src.at[:, cut], dst.at[:, cut], sems.at[n, block]))
            moves[-1].start()
    for move in moves:
        move.wait()


def merge(geo, f, c, recv):
    shape = jax.ShapeDtypeStruct(f.shape, BF16)
    return pl.pallas_call(
        functools.partial(merge_kernel, geo),
        out_specs=[pl.BlockSpec(memory_space=pl.ANY)] * 2,
        out_shape=(shape, shape),
        scratch_shapes=[pltpu.VMEM(f.shape, BF16)] * 2 + [
            pltpu.SemaphoreType.DMA((2, geo["blocks"]))],
        name="merge",
        compiler_params=params(),
        cost_estimate=cost(MERGE),
    )(f, c, recv)


def runs(geo, number, at, size):
    rows, cols, width = geo["rows"], geo["cols"], geo["width"]
    b, i = number // geo["images"], number % geo["images"]
    for cell in range(at, at + size, cols):
        line, c = cell // width, cell % width // cols
        r, y = line // rows, line % rows
        yield (b * geo["nr"] + r) * geo["nc"] + c, (i * rows + y) * cols


def read_strip(geo, recv, which, slot, number, at, size):
    cols = geo["cols"]
    return jnp.concatenate([
        recv[peer, which, slot, p : p + cols, :] for peer, p in runs(geo, number, at, size)], axis=0)


def write_strip(geo, out, number, at, value):
    cols = geo["cols"]
    for n, (peer, p) in enumerate(runs(geo, number, at, value.shape[0])):
        out[peer, p : p + cols, :] = value[n * cols : (n + 1) * cols, :]


def strips(geo):
    size = STRIP * geo["width"]
    return [(at, size) for at in range(0, geo["area"], size)]


def column_is(geo, shape, place):
    return lax.broadcasted_iota(jnp.int32, shape, 0) % geo["width"] == place


def clear_rim(geo, x2):
    width, group, area = geo["width"], geo["group"], geo["area"]
    zero = jnp.zeros((width, 2 * group), BF16)
    for n in range(geo["maps"]):
        x2[n, 0:width, :] = zero
        x2[n, width + area : 2 * width + area, :] = zero


def fill_strip(geo, x2, number, at, value):
    width, group, size = geo["width"], geo["group"], value.shape[0]
    right = pltpu.roll(value.astype(F32), size - 1, 0)
    right = jnp.where(column_is(geo, right.shape, width - 1), 0.0, right)
    rows = pl.ds(width + at, size)
    x2[number, rows, 0:group] = value.astype(BF16)
    x2[number, rows, group : 2 * group] = right.astype(BF16)


def around(geo, x2, number):
    width, area = geo["width"], geo["area"]
    return jnp.concatenate([x2[number, pl.ds(dy * width, area), :] for dy in range(3)], axis=1)


def join(geo, pair):
    group = geo["group"]
    left = pltpu.roll(pair[:, group:], 1, 0)
    return pair[:, :group] + jnp.where(column_is(geo, left.shape, 0), 0.0, left)


def forward_weights(geo, w, out):
    group = geo["group"]
    for dy in range(3):
        at = dy * 2 * group
        out[0:group, at : at + 2 * group] = w[:, (3 * dy + 1) * group : (3 * dy + 3) * group]
        out[group : 2 * group, at : at + group] = w[:, 3 * dy * group : (3 * dy + 1) * group]
        out[group : 2 * group, at + group : at + 2 * group] = jnp.zeros((group, group), BF16)


def adjoint_weights(geo, w, out):
    group = geo["group"]
    for row in range(3):
        dy, at = 2 - row, row * 2 * group
        out[at : at + group, :] = w[:, (3 * dy + 1) * group : (3 * dy + 3) * group]
        out[at + group : at + 2 * group, 0:group] = w[:, 3 * dy * group : (3 * dy + 1) * group]
        out[at + group : at + 2 * group, group : 2 * group] = jnp.zeros((group, group), BF16)


def conv(geo, x2, number, at, size, weights, turned):
    span, width = 2 * geo["group"], geo["width"]
    total = None
    for dy in range(3):
        rows = x2[number, pl.ds(at + dy * width, size), :]
        if turned:
            part = jnp.dot(
                rows, weights[dy * span : (dy + 1) * span, :], preferred_element_type=F32)
        else:
            part = lax.dot_general(
                rows, weights[:, dy * span : (dy + 1) * span], (((1,), (1,)), ((), ())),
                preferred_element_type=F32)
        total = part if total is None else total + part
    return join(geo, total)


def terms(geo, g2, x2, out):
    width, area, group = geo["width"], geo["area"], geo["group"]
    total = None
    for n in range(geo["maps"]):
        part = lax.dot_general(
            g2[n, pl.ds(width, area), :], around(geo, x2, n), (((0,), (0,)), ((), ())),
            preferred_element_type=F32)
        total = part if total is None else total + part
    for dy in range(3):
        at, to = dy * 2 * group, dy * 3 * group
        out[:, to + group : to + 3 * group] = total[0:group, at : at + 2 * group]
        out[:, to : to + group] = total[group : 2 * group, at : at + group]


def load_weights(geo, slot, refs, w):
    if not geo["pairs"]:
        w[...] = refs[0][slot]
        return
    e = lax.axis_index("de")
    half = w.shape[0] // 2
    mine = lax.axis_index("da") == slot

    def put(here, there):
        w[pl.ds(pl.multiple_of(e * half, half), half), :] = here[...]
        w[pl.ds(pl.multiple_of((1 - e) * half, half), half), :] = there[...]

    if len(refs) == 2:
        refs = [ref.at[n] for n in range(2) for ref in refs]
    pl.when(mine)(lambda: put(refs[0], refs[1]))
    pl.when(jnp.logical_not(mine))(lambda: put(refs[2], refs[3]))


def split_terms(geo, slot, total, refs):
    if not geo["pairs"]:
        refs[0][slot] = total[...]
        return
    keep_near, keep_far, send_near, send_far = refs
    e = lax.axis_index("de")
    half = keep_near.shape[0]
    mine = lax.axis_index("da") == slot

    def put(keep, send):
        keep[...] = total[pl.ds(pl.multiple_of(e * half, half), half), :]
        send[...] = total[pl.ds(pl.multiple_of((1 - e) * half, half), half), :].astype(BF16)

    pl.when(mine)(lambda: put(keep_near, send_near))
    pl.when(jnp.logical_not(mine))(lambda: put(keep_far, send_far))


def split_slots(geo, slot, total, refs):
    if not geo["pairs"]:
        refs[0][slot] = total[...]
        return
    keep, send = refs
    mine = lax.axis_index("da") == slot

    @pl.when(mine)
    def _():
        keep[...] = total[...]

    @pl.when(jnp.logical_not(mine))
    def _():
        send[...] = total[...].astype(BF16)


def term_out(geo):
    if not geo["pairs"]:
        return [jax.ShapeDtypeStruct((geo["slots"], geo["group"], geo["fan"]), F32)]
    shape = (geo["group"] // 2, geo["fan"])
    return [jax.ShapeDtypeStruct(shape, t) for t in (F32, F32, BF16, BF16)]


def slot_out(geo):
    if not geo["pairs"]:
        return term_out(geo)
    return [jax.ShapeDtypeStruct((geo["group"], geo["fan"]), t) for t in (F32, BF16)]


def map_shape(geo):
    return jax.ShapeDtypeStruct((geo["slots"], geo["maps"], geo["area"], geo["group"]), BF16)


def send_shape(geo):
    return jax.ShapeDtypeStruct(
        (geo["peers"], 2, geo["slots"], geo["piece"], geo["group"]), BF16)


def scratch(geo, pairs, total, *weights):
    fan, group, slots = geo["fan"], geo["group"], geo["slots"]
    rows = geo["area"] + 2 * geo["width"]
    shapes = [pltpu.VMEM((slots, geo["maps"], rows, 2 * group), BF16) for _ in range(pairs)]
    shapes += [pltpu.VMEM((slots,) + dims, BF16) for dims in weights]
    return shapes + ([pltpu.VMEM((slots, group, fan), F32)] if total else [])


def weight_shapes(geo):
    group = geo["group"]
    return (group, geo["fan"]), (2 * group, 6 * group), (6 * group, 2 * group)


def conv_flops(geo):
    return 2 * geo["slots"] * geo["maps"] * geo["area"] * geo["group"] * geo["fan"]


def call(geo, body, name, args, out_shape, scratch_shapes, flops):
    return pl.pallas_call(
        functools.partial(body, geo),
        out_shape=out_shape,
        scratch_shapes=scratch_shapes,
        name=name,
        compiler_params=params(),
        cost_estimate=cost(flops),
    )(*args)


def first_kernel(geo, *refs):
    nw = 2 if geo["pairs"] else 1
    recv, h_out, s_out = refs[nw : nw + 3]
    t_out, buffers = refs[nw + 3 : -6], refs[-6:]
    for slot in range(geo["slots"]):
        x2, y2, g2, w, fw, total = [ref.at[slot] for ref in buffers]
        for buffer in (x2, y2, g2):
            clear_rim(geo, buffer)
        load_weights(geo, slot, refs[:nw], w)
        forward_weights(geo, w, fw)
        for n in range(geo["maps"]):
            for at, size in strips(geo):
                fill_strip(geo, x2, n, at, read_strip(geo, recv, 0, slot, n, at, size))
                fill_strip(geo, g2, n, at, read_strip(geo, recv, 1, slot, n, at, size))
        for n in range(geo["maps"]):
            for at, size in strips(geo):
                z = conv(geo, x2, n, at, size, fw, False).astype(BF16).astype(F32)
                h, slope = act_both(z)
                h = h.astype(BF16)
                h_out[slot, n, at : at + size, :] = h
                s_out[slot, n, at : at + size, :] = slope.astype(BF16)
                fill_strip(geo, y2, n, at, h)
        terms(geo, g2, y2, total)
        split_slots(geo, slot, total, t_out)


def first(geo, one, recv):
    return call(
        geo, first_kernel, "first", (*one, recv),
        [map_shape(geo)] * 2 + slot_out(geo),
        scratch(geo, 3, True, *weight_shapes(geo)[:2]), FIRST)


def second_kernel(geo, nw, *refs):
    one, two = refs[: nw[0]], refs[nw[0] : sum(nw)]
    recv, h_in, s_in, l_out, out, *buffers, stage, sems = refs[sum(nw) :]
    moves = []

    def leave(which, slot):
        move = pltpu.make_async_copy(
            stage.at[which, slot], out.at[:, which, slot], sems.at[which, slot])
        move.start()
        moves.append(move)

    for slot in range(geo["slots"]):
        x2, y2, z2, w, fw2, aw2, aw1 = [ref.at[slot] for ref in buffers]
        for buffer in (x2, y2, z2):
            clear_rim(geo, buffer)
        load_weights(geo, slot, two, w)
        forward_weights(geo, w, fw2)
        adjoint_weights(geo, w, aw2)
        load_weights(geo, slot, one, w)
        adjoint_weights(geo, w, aw1)
        for n in range(geo["maps"]):
            for at, size in strips(geo):
                fill_strip(geo, x2, n, at, h_in[slot, n, at : at + size, :])
                fill_strip(geo, y2, n, at, read_strip(geo, recv, 1, slot, n, at, size))
        for n in range(geo["maps"]):
            for at, size in strips(geo):
                value = ALPHA * conv(geo, x2, n, at, size, fw2, False)
                write_strip(geo, stage.at[0, slot], n, at, value.astype(BF16))
        leave(0, slot)
        for n in range(geo["maps"]):
            for at, size in strips(geo):
                low = conv(geo, y2, n, at, size, aw2, True)
                low = (low * s_in[slot, n, at : at + size, :].astype(F32)).astype(BF16)
                l_out[slot, n, at : at + size, :] = low
                fill_strip(geo, z2, n, at, low)
        for n in range(geo["maps"]):
            for at, size in strips(geo):
                value = conv(geo, z2, n, at, size, aw1, True)
                write_strip(geo, stage.at[1, slot], n, at, value.astype(BF16))
        leave(1, slot)
    for move in moves:
        move.wait()


def second(geo, one, two, recv, hidden, slope):
    nw = (len(one), len(two))
    shapes = weight_shapes(geo)
    sent = send_shape(geo)
    args = (*one, *two, recv, hidden, slope)
    return pl.pallas_call(
        functools.partial(second_kernel, geo, nw),
        out_shape=[map_shape(geo), sent],
        out_specs=[
            pl.BlockSpec(memory_space=pltpu.VMEM), pl.BlockSpec(memory_space=pl.ANY)],
        scratch_shapes=scratch(geo, 3, False, *shapes, shapes[2]) + [
            pltpu.VMEM((2, geo["slots"], geo["peers"], geo["piece"], geo["group"]), BF16),
            pltpu.SemaphoreType.DMA((2, geo["slots"]))],
        name="second",
        compiler_params=params(),
        cost_estimate=cost(SECOND),
    )(*args)


def lower_kernel(geo, recv, l_in, *refs):
    t_out, buffers = refs[:-3], refs[-3:]
    for slot in range(geo["slots"]):
        x2, g2, total = [ref.at[slot] for ref in buffers]
        clear_rim(geo, x2)
        clear_rim(geo, g2)
        for n in range(geo["maps"]):
            for at, size in strips(geo):
                fill_strip(geo, x2, n, at, read_strip(geo, recv, 0, slot, n, at, size))
                fill_strip(geo, g2, n, at, l_in[slot, n, at : at + size, :])
        terms(geo, g2, x2, total)
        split_terms(geo, slot, total, t_out)


def lower(geo, recv, low):
    return call(
        geo, lower_kernel, "lower", (recv, low), term_out(geo), scratch(geo, 2, True), LOWER)


def fold_kernel(keep, recv, send):
    send[...] = (keep[...] + recv[...].astype(F32)).astype(BF16)


def fold(keep, recv):
    return pl.pallas_call(
        fold_kernel,
        out_shape=jax.ShapeDtypeStruct(keep.shape, BF16),
        name="fold",
        compiler_params=params(),
        cost_estimate=cost(FOLD),
    )(keep, recv)


def halve_kernel(keep, recv, mine, send):
    e = lax.axis_index("de")
    half = mine.shape[0]
    here = pl.ds(pl.multiple_of(e * half, half), half)
    there = pl.ds(pl.multiple_of((1 - e) * half, half), half)
    mine[...] = keep[here, :] + recv[here, :].astype(F32)
    send[...] = (keep[there, :] + recv[there, :].astype(F32)).astype(BF16)


def halve(keep, recv):
    shape = (keep.shape[0] // 2, keep.shape[1])
    return pl.pallas_call(
        halve_kernel,
        out_shape=[jax.ShapeDtypeStruct(shape, F32), jax.ShapeDtypeStruct(shape, BF16)],
        name="halve",
        compiler_params=params(),
        cost_estimate=cost(FOLD),
    )(keep, recv)


def swap(value, axis):
    return lax.ppermute(value, axis, [(0, 1), (1, 0)])


def relay_kernel(rows, over, out):
    out[0] = rows[...]
    out[1] = over[...]


def relay(rows, over):
    return pl.pallas_call(
        relay_kernel,
        out_shape=jax.ShapeDtypeStruct((2,) + rows.shape, rows.dtype),
        name="relay",
        compiler_params=params(),
        cost_estimate=cost(RELAY),
    )(rows, over)


def gather_rows(geo, one, two):
    if not geo["pairs"]:
        full = [lax.all_gather(w, ("da", "de"), axis=0, tiled=True) for w in (one, two)]
        return [(w.reshape(geo["slots"], geo["group"], geo["fan"]),) for w in full]
    over = swap(one, "da")
    two, over = lax.optimization_barrier((two, over))
    one = relay(one, over)
    near, over = swap(two, "de"), swap(two, "da")
    return (one, swap(one, "de")), (two, near, over, swap(over, "de"))


def local(group, features, cotangent, kernel_one, kernel_two, gain_one, gain_two):
    images, rows, cols, chans = features.shape
    fan = kernel_one.shape[2]
    nr, nc = lax.axis_size("row"), lax.axis_size("col")
    na, nb, ne = lax.axis_size("da"), lax.axis_size("db"), lax.axis_size("de")
    blocks = nr * nc
    geo = dict(
        group=group, fan=fan, nr=nr, nc=nc, nb=nb, blocks=blocks, slots=na,
        per_block=chans // blocks // group, peers=nb * blocks, images=images,
        rows=rows, cols=cols, piece=images * rows * cols, width=nc * cols,
        area=nr * rows * nc * cols, maps=nb * images, pairs=na == 2 and ne == 2,
    )
    flat = (images * rows * cols, chans)
    f, c = features.reshape(flat), cotangent.reshape(flat)
    k1, k2 = kernel_one.reshape(-1, fan), kernel_two.reshape(-1, fan)
    w1, w2, pieces = prep(geo, k1, k2, gain_one, gain_two, f, c)

    def exchange(x):
        return lax.all_to_all(x, ("db", "row", "col"), 0, 0, tiled=True)

    recv = exchange(pieces)
    one, two = gather_rows(geo, w1, w2)
    hidden, slope, *parts_two = first(geo, one, recv)
    low, out = second(geo, one, two, recv, hidden, slope)
    parts_one = lower(geo, recv, low)
    if geo["pairs"]:
        keep2, send2 = parts_two
        mine2, half2 = halve(keep2, swap(send2, "da"))
        keep1, far1, send1, away1 = parts_one
        back = exchange(out)
        away1, half2 = lax.optimization_barrier((swap(away1, "de"), half2))
        far1, send1 = lax.optimization_barrier((fold(far1, away1), send1))
        grad_two = pull_rows(k2, gain_two, (mine2, swap(half2, "de")), PULL)
        grad_one = pull_rows(k1, gain_one, (keep1, swap(send1, "de"), swap(far1, "da")), PULL)
    else:
        back = exchange(out)
        flat = jnp.stack([x[0].reshape(geo["slots"] * group, fan) for x in (parts_one, parts_two)])
        sums = lax.psum_scatter(flat, ("da", "de"), scatter_dimension=1, tiled=True)
        grad_one = pull_rows(k1, gain_one, (sums[0],), SMALL)
        grad_two = pull_rows(k2, gain_two, (sums[1],), SMALL)
    outputs, input_grad = merge(geo, f, c, back)
    return (
        outputs.reshape(features.shape),
        input_grad.reshape(features.shape),
        grad_one.reshape(kernel_one.shape),
        grad_two.reshape(kernel_two.shape),
    )


def solution(mesh):
    names = ("da", "db", "de", "row", "col")
    nr, nc, dp = mesh.shape["row"], mesh.shape["col"], mesh.shape["dp"]

    def run(features, cotangent, kernel_one, kernel_two, gain_one, gain_two):
        group = kernel_one.shape[2] // 9
        per_block = kernel_one.shape[1] // group
        na = 2 if per_block % 2 == 0 else 1
        nb = per_block // na
        fine = Mesh(mesh.devices.reshape(na, nb, dp // per_block, nr, nc), names)
        dps = ("da", "db", "de")
        cells = P(dps, "row", "col", None)
        rows = P(("row", "col"), dps, None)
        gains = P(("row", "col"), dps)
        return jax.shard_map(
            functools.partial(local, group),
            mesh=fine,
            in_specs=(cells, cells, rows, rows, gains, gains),
            out_specs=(cells, cells, rows, rows),
            check_vma=False,
        )(features, cotangent, kernel_one, kernel_two, gain_one, gain_two)

    return run
```

```python
import functools
import math

import jax
import jax.numpy as jnp
from jax import lax
from jax.experimental import pallas as pl
from jax.experimental.pallas import tpu as pltpu
from jax.sharding import Mesh, PartitionSpec as P

GAMMA = 1.7015043497085571
ALPHA = 0.2
EPS = 1e-06
ROOT = math.sqrt(2.0 / math.pi)
CUBE = 0.044715
F32 = jnp.float32
BF16 = jnp.bfloat16
VMEM_LIMIT = 24 * 1024 * 1024
SMALL = 1
RELAY = 20_000_000_000
FIRST = 3_000_000_000
LOWER = RELAY
SECOND = FOLD = RELAY
PULL = MERGE = SMALL
STRIP = 4


def act_value(x):
    t = jnp.tanh(x * (ROOT + (CUBE * ROOT) * (x * x)))
    return (0.5 * GAMMA) * x * (1.0 + t)


def act_slope(x):
    sq = x * x
    t = jnp.tanh(x * (ROOT + (CUBE * ROOT) * sq))
    return (0.5 * GAMMA) * ((1.0 + t) + x * (1.0 - t * t) * (ROOT + (3.0 * CUBE * ROOT) * sq))


def act_both(x):
    sq = x * x
    t = jnp.tanh(x * (ROOT + (CUBE * ROOT) * sq))
    up = 1.0 + t
    value = (0.5 * GAMMA) * x * up
    bend = x * (1.0 - t * t) * (ROOT + (3.0 * CUBE * ROOT) * sq)
    return value, (0.5 * GAMMA * ALPHA) * (up + bend)


def params(**kw):
    return pltpu.CompilerParams(vmem_limit_bytes=VMEM_LIMIT, **kw)


def pin(x):
    return pltpu.with_memory_space_constraint(x, pltpu.HBM)


def cost(flops):
    return pl.CostEstimate(flops=flops, bytes_accessed=1, transcendentals=0)


def column(gain_ref):
    rows = gain_ref.shape[1]
    first = lax.broadcasted_iota(jnp.int32, (rows, rows), 0)
    second = lax.broadcasted_iota(jnp.int32, (rows, rows), 1)
    spread = jnp.broadcast_to(gain_ref[...], (rows, rows))
    return jnp.sum(jnp.where(first == second, spread, 0.0), axis=1, keepdims=True)


def std_into(k, g, w):
    fan = k.shape[1]
    kern = k[...]
    cent = kern - jnp.mean(kern, axis=1, keepdims=True)
    var = jnp.mean(cent * cent, axis=1, keepdims=True)
    scale = column(g) * lax.rsqrt(var + EPS) * (1.0 / math.sqrt(fan))
    w[...] = (cent * scale).astype(BF16)


def pull_kernel(factor, k, g, *refs):
    out = refs[-1]
    fan = k.shape[1]
    kern = k[...]
    grad = sum(ref[...].astype(F32) for ref in refs[:-1])
    cent = kern - jnp.mean(kern, axis=1, keepdims=True)
    var = jnp.mean(cent * cent, axis=1, keepdims=True)
    inv = lax.rsqrt(var + EPS)
    scale = column(g) * inv * (factor / math.sqrt(fan))
    dot = jnp.mean(grad * cent, axis=1, keepdims=True)
    term = scale * (grad - cent * (inv * inv * dot))
    out[...] = term - jnp.mean(term, axis=1, keepdims=True)


def pull_rows(k, g, sums, factor):
    return pl.pallas_call(
        functools.partial(pull_kernel, factor),
        out_shape=jax.ShapeDtypeStruct(k.shape, F32),
        name="pull_rows",
        compiler_params=params(),
        cost_estimate=cost(PULL),
    )(k, g, *sums)


def prep_kernel(geo, k1, k2, g1, g2, f, c, w1, w2, out, *scratch):
    k1_in, k2_in, g1_in, g2_in, f_in, c_in, stage, sems, sent = scratch
    group, blocks = geo["group"], geo["blocks"]
    span = geo["per_block"] * group

    def bring(src, dst):
        move = pltpu.make_async_copy(src, dst, sems.at[len(moves)])
        moves.append(move)
        move.start()
        return move

    moves, cells = [], []
    for n in range(blocks):
        cut = pl.ds(n * span, span)
        cells.append((bring(f.at[:, cut], f_in.at[:, cut]), bring(c.at[:, cut], c_in.at[:, cut])))
        if n == 0:
            rows = [bring(*pair) for pair in ((k1, k1_in), (g1, g1_in), (k2, k2_in), (g2, g2_in))]
    leaves = []
    for block in range(blocks):
        for move in cells[block]:
            move.wait()
        for b in range(geo["nb"]):
            dst = b * blocks + block
            for slot in range(geo["slots"]):
                at = (block * geo["per_block"] + slot * geo["nb"] + b) * group
                stage[dst, 0, slot] = act_value(f_in[:, at : at + group].astype(F32)).astype(BF16)
                stage[dst, 1, slot] = c_in[:, at : at + group]
            leaves.append(pltpu.make_async_copy(stage.at[dst], out.at[dst], sent.at[dst]))
            leaves[-1].start()
        if block == 0:
            for move in rows[:2]:
                move.wait()
            std_into(k1_in, g1_in, w1)
            for move in rows[2:]:
                move.wait()
            std_into(k2_in, g2_in, w2)
    for move in leaves:
        move.wait()


def prep(geo, k1, k2, g1, g2, f, c):
    args = (k1, k2, g1, g2, f, c)
    dims = (geo["peers"], 2, geo["slots"], f.shape[0], geo["group"])
    vmem, hbm = (pl.BlockSpec(memory_space=m) for m in (pltpu.VMEM, pl.ANY))
    return pl.pallas_call(
        functools.partial(prep_kernel, geo),
        in_specs=[hbm] * 6,
        out_specs=[vmem, vmem, hbm],
        out_shape=[jax.ShapeDtypeStruct(k1.shape, BF16)] * 2 + [jax.ShapeDtypeStruct(dims, BF16)],
        scratch_shapes=[pltpu.VMEM(x.shape, x.dtype) for x in args] + [
            pltpu.VMEM(dims, BF16),
            pltpu.SemaphoreType.DMA((4 + 2 * geo["blocks"],)),
            pltpu.SemaphoreType.DMA((geo["peers"],))],
        name="prep",
        compiler_params=params(),
        cost_estimate=cost(SMALL),
    )(*[pin(x) for x in args])


def merge_kernel(geo, f, c, recv, out, grad, out_in, grad_in, sems):
    group, blocks = geo["group"], geo["blocks"]
    span = geo["per_block"] * group
    moves = []
    for block in range(blocks):
        for b in range(geo["nb"]):
            src = b * blocks + block
            for slot in range(geo["slots"]):
                at = (block * geo["per_block"] + slot * geo["nb"] + b) * group
                x = f[:, at : at + group].astype(F32)
                out_in[:, at : at + group] = (x + recv[src, 0, slot].astype(F32)).astype(BF16)
                grad_in[:, at : at + group] = (
                    c[:, at : at + group].astype(F32)
                    + act_slope(x) * recv[src, 1, slot].astype(F32)
                ).astype(BF16)
        cut = pl.ds(block * span, span)
        for n, (src, dst) in enumerate(((out_in, out), (grad_in, grad))):
            moves.append(pltpu.make_async_copy(
                src.at[:, cut], dst.at[:, cut], sems.at[n, block]))
            moves[-1].start()
    for move in moves:
        move.wait()


def merge(geo, f, c, recv):
    shape = jax.ShapeDtypeStruct(f.shape, BF16)
    return pl.pallas_call(
        functools.partial(merge_kernel, geo),
        out_specs=[pl.BlockSpec(memory_space=pl.ANY)] * 2,
        out_shape=(shape, shape),
        scratch_shapes=[pltpu.VMEM(f.shape, BF16)] * 2 + [
            pltpu.SemaphoreType.DMA((2, geo["blocks"]))],
        name="merge",
        compiler_params=params(),
        cost_estimate=cost(MERGE),
    )(f, c, recv)


def runs(geo, number, at, size):
    rows, cols, width = geo["rows"], geo["cols"], geo["width"]
    b, i = number // geo["images"], number % geo["images"]
    for cell in range(at, at + size, cols):
        line, c = cell // width, cell % width // cols
        r, y = line // rows, line % rows
        yield (b * geo["nr"] + r) * geo["nc"] + c, (i * rows + y) * cols


def read_strip(geo, recv, which, slot, number, at, size):
    cols = geo["cols"]
    return jnp.concatenate([
        recv[peer, which, slot, p : p + cols, :] for peer, p in runs(geo, number, at, size)], axis=0)


def write_strip(geo, out, number, at, value):
    cols = geo["cols"]
    for n, (peer, p) in enumerate(runs(geo, number, at, value.shape[0])):
        out[peer, p : p + cols, :] = value[n * cols : (n + 1) * cols, :]


def strips(geo):
    size = STRIP * geo["width"]
    return [(at, size) for at in range(0, geo["area"], size)]


def column_is(geo, shape, place):
    return lax.broadcasted_iota(jnp.int32, shape, 0) % geo["width"] == place


def clear_rim(geo, x2):
    width, group, area = geo["width"], geo["group"], geo["area"]
    zero = jnp.zeros((width, 2 * group), BF16)
    for n in range(geo["maps"]):
        x2[n, 0:width, :] = zero
        x2[n, width + area : 2 * width + area, :] = zero


def fill_strip(geo, x2, number, at, value):
    width, group, size = geo["width"], geo["group"], value.shape[0]
    right = pltpu.roll(value.astype(F32), size - 1, 0)
    right = jnp.where(column_is(geo, right.shape, width - 1), 0.0, right)
    rows = pl.ds(width + at, size)
    x2[number, rows, 0:group] = value.astype(BF16)
    x2[number, rows, group : 2 * group] = right.astype(BF16)


def around(geo, x2, number):
    width, area = geo["width"], geo["area"]
    return jnp.concatenate([x2[number, pl.ds(dy * width, area), :] for dy in range(3)], axis=1)


def join(geo, pair):
    group = geo["group"]
    left = pltpu.roll(pair[:, group:], 1, 0)
    return pair[:, :group] + jnp.where(column_is(geo, left.shape, 0), 0.0, left)


def forward_weights(geo, w, out):
    group = geo["group"]
    for dy in range(3):
        at = dy * 2 * group
        out[0:group, at : at + 2 * group] = w[:, (3 * dy + 1) * group : (3 * dy + 3) * group]
        out[group : 2 * group, at : at + group] = w[:, 3 * dy * group : (3 * dy + 1) * group]
        out[group : 2 * group, at + group : at + 2 * group] = jnp.zeros((group, group), BF16)


def adjoint_weights(geo, w, out):
    group = geo["group"]
    for row in range(3):
        dy, at = 2 - row, row * 2 * group
        out[at : at + group, :] = w[:, (3 * dy + 1) * group : (3 * dy + 3) * group]
        out[at + group : at + 2 * group, 0:group] = w[:, 3 * dy * group : (3 * dy + 1) * group]
        out[at + group : at + 2 * group, group : 2 * group] = jnp.zeros((group, group), BF16)


def conv(geo, x2, number, at, size, weights, turned):
    span, width = 2 * geo["group"], geo["width"]
    total = None
    for dy in range(3):
        rows = x2[number, pl.ds(at + dy * width, size), :]
        if turned:
            part = jnp.dot(
                rows, weights[dy * span : (dy + 1) * span, :], preferred_element_type=F32)
        else:
            part = lax.dot_general(
                rows, weights[:, dy * span : (dy + 1) * span], (((1,), (1,)), ((), ())),
                preferred_element_type=F32)
        total = part if total is None else total + part
    return join(geo, total)


def terms(geo, g2, x2, out):
    width, area, group = geo["width"], geo["area"], geo["group"]
    total = None
    for n in range(geo["maps"]):
        part = lax.dot_general(
            g2[n, pl.ds(width, area), :], around(geo, x2, n), (((0,), (0,)), ((), ())),
            preferred_element_type=F32)
        total = part if total is None else total + part
    for dy in range(3):
        at, to = dy * 2 * group, dy * 3 * group
        out[:, to + group : to + 3 * group] = total[0:group, at : at + 2 * group]
        out[:, to : to + group] = total[group : 2 * group, at : at + group]


def load_weights(geo, slot, refs, w):
    if not geo["pairs"]:
        w[...] = refs[0][slot]
        return
    e = lax.axis_index("de")
    half = w.shape[0] // 2
    mine = lax.axis_index("da") == slot

    def put(here, there):
        w[pl.ds(pl.multiple_of(e * half, half), half), :] = here[...]
        w[pl.ds(pl.multiple_of((1 - e) * half, half), half), :] = there[...]

    if len(refs) == 2:
        refs = [ref.at[n] for n in range(2) for ref in refs]
    pl.when(mine)(lambda: put(refs[0], refs[1]))
    pl.when(jnp.logical_not(mine))(lambda: put(refs[2], refs[3]))


def split_terms(geo, slot, total, refs):
    if not geo["pairs"]:
        refs[0][slot] = total[...]
        return
    keep_near, keep_far, send_near, send_far = refs
    e = lax.axis_index("de")
    half = keep_near.shape[0]
    mine = lax.axis_index("da") == slot

    def put(keep, send):
        keep[...] = total[pl.ds(pl.multiple_of(e * half, half), half), :]
        send[...] = total[pl.ds(pl.multiple_of((1 - e) * half, half), half), :].astype(BF16)

    pl.when(mine)(lambda: put(keep_near, send_near))
    pl.when(jnp.logical_not(mine))(lambda: put(keep_far, send_far))


def split_slots(geo, slot, total, refs):
    if not geo["pairs"]:
        refs[0][slot] = total[...]
        return
    keep, send = refs
    mine = lax.axis_index("da") == slot

    @pl.when(mine)
    def _():
        keep[...] = total[...]

    @pl.when(jnp.logical_not(mine))
    def _():
        send[...] = total[...].astype(BF16)


def term_out(geo):
    if not geo["pairs"]:
        return [jax.ShapeDtypeStruct((geo["slots"], geo["group"], geo["fan"]), F32)]
    shape = (geo["group"] // 2, geo["fan"])
    return [jax.ShapeDtypeStruct(shape, t) for t in (F32, F32, BF16, BF16)]


def slot_out(geo):
    if not geo["pairs"]:
        return term_out(geo)
    return [jax.ShapeDtypeStruct((geo["group"], geo["fan"]), t) for t in (F32, BF16)]


def map_shape(geo):
    return jax.ShapeDtypeStruct((geo["slots"], geo["maps"], geo["area"], geo["group"]), BF16)


def send_shape(geo):
    return jax.ShapeDtypeStruct(
        (geo["peers"], 2, geo["slots"], geo["piece"], geo["group"]), BF16)


def scratch(geo, pairs, total, *weights):
    fan, group, slots = geo["fan"], geo["group"], geo["slots"]
    rows = geo["area"] + 2 * geo["width"]
    shapes = [pltpu.VMEM((slots, geo["maps"], rows, 2 * group), BF16) for _ in range(pairs)]
    shapes += [pltpu.VMEM((slots,) + dims, BF16) for dims in weights]
    return shapes + ([pltpu.VMEM((slots, group, fan), F32)] if total else [])


def weight_shapes(geo):
    group = geo["group"]
    return (group, geo["fan"]), (2 * group, 6 * group), (6 * group, 2 * group)


def conv_flops(geo):
    return 2 * geo["slots"] * geo["maps"] * geo["area"] * geo["group"] * geo["fan"]


def call(geo, body, name, args, out_shape, scratch_shapes, flops):
    return pl.pallas_call(
        functools.partial(body, geo),
        out_shape=out_shape,
        scratch_shapes=scratch_shapes,
        name=name,
        compiler_params=params(),
        cost_estimate=cost(flops),
    )(*args)


def first_kernel(geo, *refs):
    nw = 2 if geo["pairs"] else 1
    recv, h_out, s_out = refs[nw : nw + 3]
    t_out, buffers = refs[nw + 3 : -6], refs[-6:]
    for slot in range(geo["slots"]):
        x2, y2, g2, w, fw, total = [ref.at[slot] for ref in buffers]
        for buffer in (x2, y2, g2):
            clear_rim(geo, buffer)
        load_weights(geo, slot, refs[:nw], w)
        forward_weights(geo, w, fw)
        for n in range(geo["maps"]):
            for at, size in strips(geo):
                fill_strip(geo, x2, n, at, read_strip(geo, recv, 0, slot, n, at, size))
                fill_strip(geo, g2, n, at, read_strip(geo, recv, 1, slot, n, at, size))
        for n in range(geo["maps"]):
            for at, size in strips(geo):
                z = conv(geo, x2, n, at, size, fw, False).astype(BF16).astype(F32)
                h, slope = act_both(z)
                h = h.astype(BF16)
                h_out[slot, n, at : at + size, :] = h
                s_out[slot, n, at : at + size, :] = slope.astype(BF16)
                fill_strip(geo, y2, n, at, h)
        terms(geo, g2, y2, total)
        split_slots(geo, slot, total, t_out)


def first(geo, one, recv):
    return call(
        geo, first_kernel, "first", (*one, recv),
        [map_shape(geo)] * 2 + slot_out(geo),
        scratch(geo, 3, True, *weight_shapes(geo)[:2]), FIRST)


def second_kernel(geo, nw, *refs):
    one, two = refs[: nw[0]], refs[nw[0] : sum(nw)]
    recv, h_in, s_in, l_out, out, *buffers, stage, sems = refs[sum(nw) :]
    moves = []

    def leave(which, slot):
        move = pltpu.make_async_copy(
            stage.at[which, slot], out.at[:, which, slot], sems.at[which, slot])
        move.start()
        moves.append(move)

    for slot in range(geo["slots"]):
        x2, y2, z2, w, fw2, aw2, aw1 = [ref.at[slot] for ref in buffers]
        for buffer in (x2, y2, z2):
            clear_rim(geo, buffer)
        load_weights(geo, slot, two, w)
        forward_weights(geo, w, fw2)
        adjoint_weights(geo, w, aw2)
        load_weights(geo, slot, one, w)
        adjoint_weights(geo, w, aw1)
        for n in range(geo["maps"]):
            for at, size in strips(geo):
                fill_strip(geo, x2, n, at, h_in[slot, n, at : at + size, :])
                fill_strip(geo, y2, n, at, read_strip(geo, recv, 1, slot, n, at, size))
        for n in range(geo["maps"]):
            for at, size in strips(geo):
                value = ALPHA * conv(geo, x2, n, at, size, fw2, False)
                write_strip(geo, stage.at[0, slot], n, at, value.astype(BF16))
        leave(0, slot)
        for n in range(geo["maps"]):
            for at, size in strips(geo):
                low = conv(geo, y2, n, at, size, aw2, True)
                low = (low * s_in[slot, n, at : at + size, :].astype(F32)).astype(BF16)
                l_out[slot, n, at : at + size, :] = low
                fill_strip(geo, z2, n, at, low)
        for n in range(geo["maps"]):
            for at, size in strips(geo):
                value = conv(geo, z2, n, at, size, aw1, True)
                write_strip(geo, stage.at[1, slot], n, at, value.astype(BF16))
        leave(1, slot)
    for move in moves:
        move.wait()


def second(geo, one, two, recv, hidden, slope):
    nw = (len(one), len(two))
    shapes = weight_shapes(geo)
    sent = send_shape(geo)
    args = (*one, *two, recv, hidden, slope)
    return pl.pallas_call(
        functools.partial(second_kernel, geo, nw),
        out_shape=[map_shape(geo), sent],
        out_specs=[
            pl.BlockSpec(memory_space=pltpu.VMEM), pl.BlockSpec(memory_space=pl.ANY)],
        scratch_shapes=scratch(geo, 3, False, *shapes, shapes[2]) + [
            pltpu.VMEM((2, geo["slots"], geo["peers"], geo["piece"], geo["group"]), BF16),
            pltpu.SemaphoreType.DMA((2, geo["slots"]))],
        name="second",
        compiler_params=params(),
        cost_estimate=cost(SECOND),
    )(*args)


def lower_kernel(geo, recv, l_in, *refs):
    t_out, buffers = refs[:-3], refs[-3:]
    for slot in range(geo["slots"]):
        x2, g2, total = [ref.at[slot] for ref in buffers]
        clear_rim(geo, x2)
        clear_rim(geo, g2)
        for n in range(geo["maps"]):
            for at, size in strips(geo):
                fill_strip(geo, x2, n, at, read_strip(geo, recv, 0, slot, n, at, size))
                fill_strip(geo, g2, n, at, l_in[slot, n, at : at + size, :])
        terms(geo, g2, x2, total)
        split_terms(geo, slot, total, t_out)


def lower(geo, recv, low):
    return call(
        geo, lower_kernel, "lower", (recv, low), term_out(geo), scratch(geo, 2, True), LOWER)


def fold_kernel(keep, recv, send):
    send[...] = (keep[...] + recv[...].astype(F32)).astype(BF16)


def fold(keep, recv):
    return pl.pallas_call(
        fold_kernel,
        out_shape=jax.ShapeDtypeStruct(keep.shape, BF16),
        name="fold",
        compiler_params=params(),
        cost_estimate=cost(FOLD),
    )(keep, recv)


def halve_kernel(keep, recv, mine, send):
    e = lax.axis_index("de")
    half = mine.shape[0]
    here = pl.ds(pl.multiple_of(e * half, half), half)
    there = pl.ds(pl.multiple_of((1 - e) * half, half), half)
    mine[...] = keep[here, :] + recv[here, :].astype(F32)
    send[...] = (keep[there, :] + recv[there, :].astype(F32)).astype(BF16)


def halve(keep, recv):
    shape = (keep.shape[0] // 2, keep.shape[1])
    return pl.pallas_call(
        halve_kernel,
        out_shape=[jax.ShapeDtypeStruct(shape, F32), jax.ShapeDtypeStruct(shape, BF16)],
        name="halve",
        compiler_params=params(),
        cost_estimate=cost(FOLD),
    )(keep, recv)


def swap(value, axis):
    return lax.ppermute(value, axis, [(0, 1), (1, 0)])


def relay_kernel(rows, over, out):
    out[0] = rows[...]
    out[1] = over[...]


def relay(rows, over):
    return pl.pallas_call(
        relay_kernel,
        out_shape=jax.ShapeDtypeStruct((2,) + rows.shape, rows.dtype),
        name="relay",
        compiler_params=params(),
        cost_estimate=cost(RELAY),
    )(rows, over)


def gather_rows(geo, one, two):
    if not geo["pairs"]:
        full = [lax.all_gather(w, ("da", "de"), axis=0, tiled=True) for w in (one, two)]
        return [(w.reshape(geo["slots"], geo["group"], geo["fan"]),) for w in full]
    over = swap(one, "da")
    two, over = lax.optimization_barrier((two, over))
    one = relay(one, over)
    near, over = swap(two, "de"), swap(two, "da")
    return (one, swap(one, "de")), (two, near, over, swap(over, "de"))


def local(group, features, cotangent, kernel_one, kernel_two, gain_one, gain_two):
    images, rows, cols, chans = features.shape
    fan = kernel_one.shape[2]
    nr, nc = lax.axis_size("row"), lax.axis_size("col")
    na, nb, ne = lax.axis_size("da"), lax.axis_size("db"), lax.axis_size("de")
    blocks = nr * nc
    geo = dict(
        group=group, fan=fan, nr=nr, nc=nc, nb=nb, blocks=blocks, slots=na,
        per_block=chans // blocks // group, peers=nb * blocks, images=images,
        rows=rows, cols=cols, piece=images * rows * cols, width=nc * cols,
        area=nr * rows * nc * cols, maps=nb * images, pairs=na == 2 and ne == 2,
    )
    flat = (images * rows * cols, chans)
    f, c = features.reshape(flat), cotangent.reshape(flat)
    k1, k2 = kernel_one.reshape(-1, fan), kernel_two.reshape(-1, fan)
    w1, w2, pieces = prep(geo, k1, k2, gain_one, gain_two, f, c)

    def exchange(x):
        return lax.all_to_all(x, ("db", "row", "col"), 0, 0, tiled=True)

    recv = exchange(pieces)
    one, two = gather_rows(geo, w1, w2)
    hidden, slope, *parts_two = first(geo, one, recv)
    low, out = second(geo, one, two, recv, hidden, slope)
    parts_one = lower(geo, recv, low)
    if geo["pairs"]:
        keep2, send2 = parts_two
        mine2, half2 = halve(keep2, swap(send2, "da"))
        keep1, far1, send1, away1 = parts_one
        back = exchange(out)
        away1, half2 = lax.optimization_barrier((swap(away1, "de"), half2))
        far1, send1 = lax.optimization_barrier((fold(far1, away1), send1))
        grad_two = pull_rows(k2, gain_two, (mine2, swap(half2, "de")), ALPHA)
        grad_one = pull_rows(k1, gain_one, (keep1, swap(send1, "de"), swap(far1, "da")), 1.0)
    else:
        back = exchange(out)
        flat = jnp.stack([x[0].reshape(geo["slots"] * group, fan) for x in (parts_one, parts_two)])
        sums = lax.psum_scatter(flat, ("da", "de"), scatter_dimension=1, tiled=True)
        grad_one = pull_rows(k1, gain_one, (sums[0],), 1.0)
        grad_two = pull_rows(k2, gain_two, (sums[1],), ALPHA)
    outputs, input_grad = merge(geo, f, c, back)
    return (
        outputs.reshape(features.shape),
        input_grad.reshape(features.shape),
        grad_one.reshape(kernel_one.shape),
        grad_two.reshape(kernel_two.shape),
    )


def solution(mesh):
    names = ("da", "db", "de", "row", "col")
    nr, nc, dp = mesh.shape["row"], mesh.shape["col"], mesh.shape["dp"]

    def run(features, cotangent, kernel_one, kernel_two, gain_one, gain_two):
        group = kernel_one.shape[2] // 9
        per_block = kernel_one.shape[1] // group
        na = 2 if per_block % 2 == 0 else 1
        nb = per_block // na
        fine = Mesh(mesh.devices.reshape(na, nb, dp // per_block, nr, nc), names)
        dps = ("da", "db", "de")
        cells = P(dps, "row", "col", None)
        rows = P(("row", "col"), dps, None)
        gains = P(("row", "col"), dps)
        return jax.shard_map(
            functools.partial(local, group),
            mesh=fine,
            in_specs=(cells, cells, rows, rows, gains, gains),
            out_specs=(cells, cells, rows, rows),
            check_vma=False,
        )(features, cotangent, kernel_one, kernel_two, gain_one, gain_two)

    return run
```

```python
import functools
import math

import jax
import jax.numpy as jnp
from jax import lax
from jax.experimental import pallas as pl
from jax.experimental.pallas import tpu as pltpu
from jax.sharding import Mesh, PartitionSpec as P

GAMMA = 1.7015043497085571
ALPHA = 0.2
EPS = 1e-06
ROOT = math.sqrt(2.0 / math.pi)
CUBE = 0.044715
F32 = jnp.float32
BF16 = jnp.bfloat16
VMEM_LIMIT = 24 * 1024 * 1024
SMALL = 1
RELAY = 20_000_000_000
FIRST = 3_000_000_000
LOWER = RELAY
SECOND = RELAY
FOLD = 1
HALVE = 1
ADD = 500_000_000
PULL = MERGE = SMALL
STRIP = 4


def act_value(x):
    t = jnp.tanh(x * (ROOT + (CUBE * ROOT) * (x * x)))
    return (0.5 * GAMMA) * x * (1.0 + t)


def act_slope(x):
    sq = x * x
    t = jnp.tanh(x * (ROOT + (CUBE * ROOT) * sq))
    return (0.5 * GAMMA) * ((1.0 + t) + x * (1.0 - t * t) * (ROOT + (3.0 * CUBE * ROOT) * sq))


def act_both(x):
    sq = x * x
    t = jnp.tanh(x * (ROOT + (CUBE * ROOT) * sq))
    up = 1.0 + t
    value = (0.5 * GAMMA) * x * up
    bend = x * (1.0 - t * t) * (ROOT + (3.0 * CUBE * ROOT) * sq)
    return value, (0.5 * GAMMA * ALPHA) * (up + bend)


def params(**kw):
    return pltpu.CompilerParams(vmem_limit_bytes=VMEM_LIMIT, **kw)


def pin(x):
    return pltpu.with_memory_space_constraint(x, pltpu.HBM)


def cost(flops):
    return pl.CostEstimate(flops=flops, bytes_accessed=1, transcendentals=0)


def column(gain_ref):
    rows = gain_ref.shape[1]
    first = lax.broadcasted_iota(jnp.int32, (rows, rows), 0)
    second = lax.broadcasted_iota(jnp.int32, (rows, rows), 1)
    spread = jnp.broadcast_to(gain_ref[...], (rows, rows))
    return jnp.sum(jnp.where(first == second, spread, 0.0), axis=1, keepdims=True)


def std_into(k, g, w):
    fan = k.shape[1]
    kern = k[...]
    cent = kern - jnp.mean(kern, axis=1, keepdims=True)
    var = jnp.mean(cent * cent, axis=1, keepdims=True)
    scale = column(g) * lax.rsqrt(var + EPS) * (1.0 / math.sqrt(fan))
    w[...] = (cent * scale).astype(BF16)


def pull_kernel(k1, k2, g1, g2, *refs):
    *sums, out1, out2 = refs
    half = len(sums) // 2
    for k, g, parts, out, factor in (
            (k1, g1, sums[:half], out1, 1.0), (k2, g2, sums[half:], out2, ALPHA)):
        fan = k.shape[1]
        kern = k[...]
        grad = sum(ref[...].astype(F32) for ref in parts)
        cent = kern - jnp.mean(kern, axis=1, keepdims=True)
        var = jnp.mean(cent * cent, axis=1, keepdims=True)
        inv = lax.rsqrt(var + EPS)
        scale = column(g) * inv * (factor / math.sqrt(fan))
        dot = jnp.mean(grad * cent, axis=1, keepdims=True)
        term = scale * (grad - cent * (inv * inv * dot))
        out[...] = term - jnp.mean(term, axis=1, keepdims=True)


def pull_rows(k1, k2, g1, g2, *sums):
    return pl.pallas_call(
        pull_kernel,
        out_shape=[jax.ShapeDtypeStruct(k1.shape, F32)] * 2,
        name="pull_rows",
        compiler_params=params(),
        cost_estimate=cost(PULL),
    )(k1, k2, g1, g2, *sums)


def prep_kernel(geo, k1, k2, g1, g2, f, c, w1, w2, out, *scratch):
    k1_in, k2_in, g1_in, g2_in, f_in, c_in, stage, sems, sent = scratch
    group, blocks = geo["group"], geo["blocks"]
    span = geo["per_block"] * group

    def bring(src, dst):
        move = pltpu.make_async_copy(src, dst, sems.at[len(moves)])
        moves.append(move)
        move.start()
        return move

    moves, cells = [], []
    for n in range(blocks):
        cut = pl.ds(n * span, span)
        cells.append((bring(f.at[:, cut], f_in.at[:, cut]), bring(c.at[:, cut], c_in.at[:, cut])))
        if n == 0:
            rows = [bring(*pair) for pair in ((k1, k1_in), (g1, g1_in), (k2, k2_in), (g2, g2_in))]
    leaves = []
    for block in range(blocks):
        for move in cells[block]:
            move.wait()
        for b in range(geo["nb"]):
            dst = b * blocks + block
            for slot in range(geo["slots"]):
                at = (block * geo["per_block"] + slot * geo["nb"] + b) * group
                stage[dst, 0, slot] = act_value(f_in[:, at : at + group].astype(F32)).astype(BF16)
                stage[dst, 1, slot] = c_in[:, at : at + group]
            leaves.append(pltpu.make_async_copy(stage.at[dst], out.at[dst], sent.at[dst]))
            leaves[-1].start()
        if block == 0:
            for move in rows[:2]:
                move.wait()
            std_into(k1_in, g1_in, w1)
            for move in rows[2:]:
                move.wait()
            std_into(k2_in, g2_in, w2)
    for move in leaves:
        move.wait()


def prep(geo, k1, k2, g1, g2, f, c):
    args = (k1, k2, g1, g2, f, c)
    dims = (geo["peers"], 2, geo["slots"], f.shape[0], geo["group"])
    vmem, hbm = (pl.BlockSpec(memory_space=m) for m in (pltpu.VMEM, pl.ANY))
    return pl.pallas_call(
        functools.partial(prep_kernel, geo),
        in_specs=[hbm] * 6,
        out_specs=[vmem, vmem, hbm],
        out_shape=[jax.ShapeDtypeStruct(k1.shape, BF16)] * 2 + [jax.ShapeDtypeStruct(dims, BF16)],
        scratch_shapes=[pltpu.VMEM(x.shape, x.dtype) for x in args] + [
            pltpu.VMEM(dims, BF16),
            pltpu.SemaphoreType.DMA((4 + 2 * geo["blocks"],)),
            pltpu.SemaphoreType.DMA((geo["peers"],))],
        name="prep",
        compiler_params=params(),
        cost_estimate=cost(SMALL),
    )(*[pin(x) for x in args])


def merge_kernel(geo, f, c, recv, out, grad, out_in, grad_in, sems):
    group, blocks = geo["group"], geo["blocks"]
    span = geo["per_block"] * group
    moves = []
    for block in range(blocks):
        for b in range(geo["nb"]):
            src = b * blocks + block
            for slot in range(geo["slots"]):
                at = (block * geo["per_block"] + slot * geo["nb"] + b) * group
                x = f[:, at : at + group].astype(F32)
                out_in[:, at : at + group] = (x + recv[src, 0, slot].astype(F32)).astype(BF16)
                grad_in[:, at : at + group] = (
                    c[:, at : at + group].astype(F32)
                    + act_slope(x) * recv[src, 1, slot].astype(F32)
                ).astype(BF16)
        cut = pl.ds(block * span, span)
        for n, (src, dst) in enumerate(((out_in, out), (grad_in, grad))):
            moves.append(pltpu.make_async_copy(
                src.at[:, cut], dst.at[:, cut], sems.at[n, block]))
            moves[-1].start()
    for move in moves:
        move.wait()


def merge(geo, f, c, recv):
    shape = jax.ShapeDtypeStruct(f.shape, BF16)
    return pl.pallas_call(
        functools.partial(merge_kernel, geo),
        out_specs=[pl.BlockSpec(memory_space=pl.ANY)] * 2,
        out_shape=(shape, shape),
        scratch_shapes=[pltpu.VMEM(f.shape, BF16)] * 2 + [
            pltpu.SemaphoreType.DMA((2, geo["blocks"]))],
        name="merge",
        compiler_params=params(),
        cost_estimate=cost(MERGE),
    )(f, c, recv)


def runs(geo, number, at, size):
    rows, cols, width = geo["rows"], geo["cols"], geo["width"]
    b, i = number // geo["images"], number % geo["images"]
    for cell in range(at, at + size, cols):
        line, c = cell // width, cell % width // cols
        r, y = line // rows, line % rows
        yield (b * geo["nr"] + r) * geo["nc"] + c, (i * rows + y) * cols


def read_strip(geo, recv, which, slot, number, at, size):
    cols = geo["cols"]
    return jnp.concatenate([
        recv[peer, which, slot, p : p + cols, :] for peer, p in runs(geo, number, at, size)], axis=0)


def write_strip(geo, out, number, at, value):
    cols = geo["cols"]
    for n, (peer, p) in enumerate(runs(geo, number, at, value.shape[0])):
        out[peer, p : p + cols, :] = value[n * cols : (n + 1) * cols, :]


def strips(geo):
    size = STRIP * geo["width"]
    return [(at, size) for at in range(0, geo["area"], size)]


def column_is(geo, shape, place):
    return lax.broadcasted_iota(jnp.int32, shape, 0) % geo["width"] == place


def clear_rim(geo, x2):
    width, group, area = geo["width"], geo["group"], geo["area"]
    zero = jnp.zeros((width, 2 * group), BF16)
    for n in range(geo["maps"]):
        x2[n, 0:width, :] = zero
        x2[n, width + area : 2 * width + area, :] = zero


def fill_strip(geo, x2, number, at, value):
    width, group, size = geo["width"], geo["group"], value.shape[0]
    right = pltpu.roll(value.astype(F32), size - 1, 0)
    right = jnp.where(column_is(geo, right.shape, width - 1), 0.0, right)
    rows = pl.ds(width + at, size)
    x2[number, rows, 0:group] = value.astype(BF16)
    x2[number, rows, group : 2 * group] = right.astype(BF16)


def around(geo, x2, number):
    width, area = geo["width"], geo["area"]
    return jnp.concatenate([x2[number, pl.ds(dy * width, area), :] for dy in range(3)], axis=1)


def join(geo, pair):
    group = geo["group"]
    left = pltpu.roll(pair[:, group:], 1, 0)
    return pair[:, :group] + jnp.where(column_is(geo, left.shape, 0), 0.0, left)


def forward_weights(geo, w, out):
    group = geo["group"]
    for dy in range(3):
        at = dy * 2 * group
        out[0:group, at : at + 2 * group] = w[:, (3 * dy + 1) * group : (3 * dy + 3) * group]
        out[group : 2 * group, at : at + group] = w[:, 3 * dy * group : (3 * dy + 1) * group]
        out[group : 2 * group, at + group : at + 2 * group] = jnp.zeros((group, group), BF16)


def adjoint_weights(geo, w, out):
    group = geo["group"]
    for row in range(3):
        dy, at = 2 - row, row * 2 * group
        out[at : at + group, :] = w[:, (3 * dy + 1) * group : (3 * dy + 3) * group]
        out[at + group : at + 2 * group, 0:group] = w[:, 3 * dy * group : (3 * dy + 1) * group]
        out[at + group : at + 2 * group, group : 2 * group] = jnp.zeros((group, group), BF16)


def conv(geo, x2, number, at, size, weights, turned):
    span, width = 2 * geo["group"], geo["width"]
    total = None
    for dy in range(3):
        rows = x2[number, pl.ds(at + dy * width, size), :]
        if turned:
            part = jnp.dot(
                rows, weights[dy * span : (dy + 1) * span, :], preferred_element_type=F32)
        else:
            part = lax.dot_general(
                rows, weights[:, dy * span : (dy + 1) * span], (((1,), (1,)), ((), ())),
                preferred_element_type=F32)
        total = part if total is None else total + part
    return join(geo, total)


def terms(geo, g2, x2, out):
    width, area, group = geo["width"], geo["area"], geo["group"]
    total = None
    for n in range(geo["maps"]):
        part = lax.dot_general(
            g2[n, pl.ds(width, area), :], around(geo, x2, n), (((0,), (0,)), ((), ())),
            preferred_element_type=F32)
        total = part if total is None else total + part
    for dy in range(3):
        at, to = dy * 2 * group, dy * 3 * group
        out[:, to + group : to + 3 * group] = total[0:group, at : at + 2 * group]
        out[:, to : to + group] = total[group : 2 * group, at : at + group]


def load_weights(geo, slot, refs, w):
    if not geo["pairs"]:
        w[...] = refs[0][slot]
        return
    e = lax.axis_index("de")
    half = w.shape[0] // 2
    mine = lax.axis_index("da") == slot

    def put(here, there):
        w[pl.ds(pl.multiple_of(e * half, half), half), :] = here[...]
        w[pl.ds(pl.multiple_of((1 - e) * half, half), half), :] = there[...]

    if len(refs) == 2:
        refs = [ref.at[n] for n in range(2) for ref in refs]
    pl.when(mine)(lambda: put(refs[0], refs[1]))
    pl.when(jnp.logical_not(mine))(lambda: put(refs[2], refs[3]))


def split_terms(geo, slot, total, refs):
    if not geo["pairs"]:
        refs[0][slot] = total[...]
        return
    keep_near, keep_far, send_near, send_far = refs
    e = lax.axis_index("de")
    half = keep_near.shape[0]
    mine = lax.axis_index("da") == slot

    def put(keep, send):
        keep[...] = total[pl.ds(pl.multiple_of(e * half, half), half), :]
        send[...] = total[pl.ds(pl.multiple_of((1 - e) * half, half), half), :].astype(BF16)

    pl.when(mine)(lambda: put(keep_near, send_near))
    pl.when(jnp.logical_not(mine))(lambda: put(keep_far, send_far))


def split_slots(geo, slot, total, refs):
    if not geo["pairs"]:
        refs[0][slot] = total[...]
        return
    keep, send = refs
    mine = lax.axis_index("da") == slot

    @pl.when(mine)
    def _():
        keep[...] = total[...]

    @pl.when(jnp.logical_not(mine))
    def _():
        send[...] = total[...].astype(BF16)


def term_out(geo):
    if not geo["pairs"]:
        return [jax.ShapeDtypeStruct((geo["slots"], geo["group"], geo["fan"]), F32)]
    shape = (geo["group"] // 2, geo["fan"])
    return [jax.ShapeDtypeStruct(shape, t) for t in (F32, F32, BF16, BF16)]


def slot_out(geo):
    if not geo["pairs"]:
        return term_out(geo)
    return [jax.ShapeDtypeStruct((geo["group"], geo["fan"]), t) for t in (F32, BF16)]


def map_shape(geo):
    return jax.ShapeDtypeStruct((geo["slots"], geo["maps"], geo["area"], geo["group"]), BF16)


def send_shape(geo):
    return jax.ShapeDtypeStruct(
        (geo["peers"], 2, geo["slots"], geo["piece"], geo["group"]), BF16)


def scratch(geo, pairs, total, *weights):
    fan, group, slots = geo["fan"], geo["group"], geo["slots"]
    rows = geo["area"] + 2 * geo["width"]
    shapes = [pltpu.VMEM((slots, geo["maps"], rows, 2 * group), BF16) for _ in range(pairs)]
    shapes += [pltpu.VMEM((slots,) + dims, BF16) for dims in weights]
    return shapes + ([pltpu.VMEM((slots, group, fan), F32)] if total else [])


def weight_shapes(geo):
    group = geo["group"]
    return (group, geo["fan"]), (2 * group, 6 * group), (6 * group, 2 * group)


def conv_flops(geo):
    return 2 * geo["slots"] * geo["maps"] * geo["area"] * geo["group"] * geo["fan"]


def call(geo, body, name, args, out_shape, scratch_shapes, flops):
    return pl.pallas_call(
        functools.partial(body, geo),
        out_shape=out_shape,
        scratch_shapes=scratch_shapes,
        name=name,
        compiler_params=params(),
        cost_estimate=cost(flops),
    )(*args)


def first_kernel(geo, *refs):
    nw = 2 if geo["pairs"] else 1
    recv, h_out, s_out = refs[nw : nw + 3]
    t_out, buffers = refs[nw + 3 : -6], refs[-6:]
    for slot in range(geo["slots"]):
        x2, y2, g2, w, fw, total = [ref.at[slot] for ref in buffers]
        for buffer in (x2, y2, g2):
            clear_rim(geo, buffer)
        load_weights(geo, slot, refs[:nw], w)
        forward_weights(geo, w, fw)
        for n in range(geo["maps"]):
            for at, size in strips(geo):
                fill_strip(geo, x2, n, at, read_strip(geo, recv, 0, slot, n, at, size))
                fill_strip(geo, g2, n, at, read_strip(geo, recv, 1, slot, n, at, size))
        for n in range(geo["maps"]):
            for at, size in strips(geo):
                z = conv(geo, x2, n, at, size, fw, False).astype(BF16).astype(F32)
                h, slope = act_both(z)
                h = h.astype(BF16)
                h_out[slot, n, at : at + size, :] = h
                s_out[slot, n, at : at + size, :] = slope.astype(BF16)
                fill_strip(geo, y2, n, at, h)
        terms(geo, g2, y2, total)
        split_slots(geo, slot, total, t_out)


def first(geo, one, recv):
    return call(
        geo, first_kernel, "first", (*one, recv),
        [map_shape(geo)] * 2 + slot_out(geo),
        scratch(geo, 3, True, *weight_shapes(geo)[:2]), FIRST)


def second_kernel(geo, nw, *refs):
    one, two = refs[: nw[0]], refs[nw[0] : sum(nw)]
    recv, h_in, s_in, l_out, out, *buffers, low_in, stage, sems, low_sems = refs[sum(nw) :]
    moves = []

    def leave(which, slot):
        move = pltpu.make_async_copy(
            stage.at[which, slot], out.at[:, which, slot], sems.at[which, slot])
        move.start()
        moves.append(move)

    for slot in range(geo["slots"]):
        x2, y2, z2, w, fw2, aw2, aw1 = [ref.at[slot] for ref in buffers]
        for buffer in (x2, y2, z2):
            clear_rim(geo, buffer)
        load_weights(geo, slot, two, w)
        forward_weights(geo, w, fw2)
        adjoint_weights(geo, w, aw2)
        load_weights(geo, slot, one, w)
        adjoint_weights(geo, w, aw1)
        for n in range(geo["maps"]):
            for at, size in strips(geo):
                fill_strip(geo, x2, n, at, h_in[slot, n, at : at + size, :])
                fill_strip(geo, y2, n, at, read_strip(geo, recv, 1, slot, n, at, size))
        for n in range(geo["maps"]):
            for at, size in strips(geo):
                value = ALPHA * conv(geo, x2, n, at, size, fw2, False)
                write_strip(geo, stage.at[0, slot], n, at, value.astype(BF16))
        leave(0, slot)
        for n in range(geo["maps"]):
            for at, size in strips(geo):
                low = conv(geo, y2, n, at, size, aw2, True)
                low = (low * s_in[slot, n, at : at + size, :].astype(F32)).astype(BF16)
                low_in[slot, n, at : at + size, :] = low
                fill_strip(geo, z2, n, at, low)
        moves.append(pltpu.make_async_copy(low_in.at[slot], l_out.at[slot], low_sems.at[slot]))
        moves[-1].start()
        for n in range(geo["maps"]):
            for at, size in strips(geo):
                value = conv(geo, z2, n, at, size, aw1, True)
                write_strip(geo, stage.at[1, slot], n, at, value.astype(BF16))
        leave(1, slot)
    for move in moves:
        move.wait()


def second(geo, one, two, recv, hidden, slope):
    nw = (len(one), len(two))
    shapes = weight_shapes(geo)
    sent = send_shape(geo)
    args = (*one, *two, recv, hidden, slope)
    return pl.pallas_call(
        functools.partial(second_kernel, geo, nw),
        out_shape=[pltpu.HBM(map_shape(geo).shape, BF16), sent],
        out_specs=[pl.BlockSpec(memory_space=pl.ANY)] * 2,
        scratch_shapes=scratch(geo, 3, False, *shapes, shapes[2]) + [
            pltpu.VMEM(map_shape(geo).shape, BF16),
            pltpu.VMEM((2, geo["slots"], geo["peers"], geo["piece"], geo["group"]), BF16),
            pltpu.SemaphoreType.DMA((2, geo["slots"])),
            pltpu.SemaphoreType.DMA((geo["slots"],))],
        name="second",
        compiler_params=params(),
        cost_estimate=cost(SECOND),
    )(*args)


def lower_kernel(geo, recv, low, k1, k2, g1, g2, *refs):
    t_out, (*buffers, l_in, sems, k_sems) = refs[:-6], refs[-6:]
    t_out, held = t_out[:-4], t_out[-4:]
    brought = [pltpu.make_async_copy(src, dst, k_sems.at[n])
               for n, (src, dst) in enumerate(zip((k1, k2, g1, g2), held))]
    slots = range(geo["slots"])
    moves = [pltpu.make_async_copy(low.at[slot], l_in.at[slot], sems.at[slot]) for slot in slots]
    for move in moves + brought:
        move.start()
    for slot in slots:
        x2 = buffers[0].at[slot]
        clear_rim(geo, x2)
        for n in range(geo["maps"]):
            for at, size in strips(geo):
                fill_strip(geo, x2, n, at, read_strip(geo, recv, 0, slot, n, at, size))
    for slot in slots:
        x2, g2, total = [ref.at[slot] for ref in buffers]
        moves[slot].wait()
        for n in range(geo["maps"]):
            for at, size in strips(geo):
                fill_strip(geo, g2, n, at, l_in[slot, n, at : at + size, :])
        terms(geo, g2, x2, total)
        split_terms(geo, slot, total, t_out)
    for move in brought:
        move.wait()


def lower(geo, recv, low, *kernels):
    vmem, hbm = (pl.BlockSpec(memory_space=m) for m in (pltpu.VMEM, pl.ANY))
    return pl.pallas_call(
        functools.partial(lower_kernel, geo),
        in_specs=[vmem] + [hbm] * 5,
        out_shape=term_out(geo) + [jax.ShapeDtypeStruct(x.shape, F32) for x in kernels],
        scratch_shapes=scratch(geo, 2, True) + [
            pltpu.VMEM(map_shape(geo).shape, BF16), pltpu.SemaphoreType.DMA((geo["slots"],)),
            pltpu.SemaphoreType.DMA((4,))],
        name="lower",
        compiler_params=params(),
        cost_estimate=cost(LOWER),
    )(recv, pin(low), *[pin(x) for x in kernels])


def fold_kernel(keep, recv, send):
    send[...] = (keep[...] + recv[...].astype(F32)).astype(BF16)


def fold(keep, recv):
    return pl.pallas_call(
        fold_kernel,
        out_shape=jax.ShapeDtypeStruct(keep.shape, BF16),
        name="fold",
        compiler_params=params(),
        cost_estimate=cost(FOLD),
    )(keep, recv)


def halve_kernel(keep, recv, mine, send):
    e = lax.axis_index("de")
    half = mine.shape[0]
    here = pl.ds(pl.multiple_of(e * half, half), half)
    there = pl.ds(pl.multiple_of((1 - e) * half, half), half)
    mine[...] = keep[here, :] + recv[here, :].astype(F32)
    send[...] = (keep[there, :] + recv[there, :].astype(F32)).astype(BF16)


def halve(keep, recv):
    shape = (keep.shape[0] // 2, keep.shape[1])
    return pl.pallas_call(
        halve_kernel,
        out_shape=[jax.ShapeDtypeStruct(shape, F32), jax.ShapeDtypeStruct(shape, BF16)],
        name="halve",
        compiler_params=params(),
        cost_estimate=cost(HALVE),
    )(keep, recv)


def add_kernel(keep, recv, out):
    out[...] = keep[...] + recv[...].astype(F32)


def add(keep, recv):
    return pl.pallas_call(
        add_kernel,
        out_shape=jax.ShapeDtypeStruct(keep.shape, F32),
        name="add",
        compiler_params=params(),
        cost_estimate=cost(ADD),
    )(keep, recv)


def swap(value, axis):
    return lax.ppermute(value, axis, [(0, 1), (1, 0)])


def relay_kernel(rows, over, out):
    out[0] = rows[...]
    out[1] = over[...]


def relay(rows, over):
    return pl.pallas_call(
        relay_kernel,
        out_shape=jax.ShapeDtypeStruct((2,) + rows.shape, rows.dtype),
        name="relay",
        compiler_params=params(),
        cost_estimate=cost(RELAY),
    )(rows, over)


def gather_rows(geo, one, two):
    if not geo["pairs"]:
        full = [lax.all_gather(w, ("da", "de"), axis=0, tiled=True) for w in (one, two)]
        return [(w.reshape(geo["slots"], geo["group"], geo["fan"]),) for w in full]
    over = swap(one, "da")
    two, over = lax.optimization_barrier((two, over))
    one = relay(one, over)
    near, over = swap(two, "de"), swap(two, "da")
    return (one, swap(one, "de")), (two, near, over, swap(over, "de"))


def local(group, features, cotangent, kernel_one, kernel_two, gain_one, gain_two):
    images, rows, cols, chans = features.shape
    fan = kernel_one.shape[2]
    nr, nc = lax.axis_size("row"), lax.axis_size("col")
    na, nb, ne = lax.axis_size("da"), lax.axis_size("db"), lax.axis_size("de")
    blocks = nr * nc
    geo = dict(
        group=group, fan=fan, nr=nr, nc=nc, nb=nb, blocks=blocks, slots=na,
        per_block=chans // blocks // group, peers=nb * blocks, images=images,
        rows=rows, cols=cols, piece=images * rows * cols, width=nc * cols,
        area=nr * rows * nc * cols, maps=nb * images, pairs=na == 2 and ne == 2,
    )
    flat = (images * rows * cols, chans)
    f, c = features.reshape(flat), cotangent.reshape(flat)
    k1, k2 = kernel_one.reshape(-1, fan), kernel_two.reshape(-1, fan)
    w1, w2, pieces = prep(geo, k1, k2, gain_one, gain_two, f, c)

    def exchange(x):
        return lax.all_to_all(x, ("db", "row", "col"), 0, 0, tiled=True)

    recv = exchange(pieces)
    one, two = gather_rows(geo, w1, w2)
    hidden, slope, *parts_two = first(geo, one, recv)
    low, out = second(geo, one, two, recv, hidden, slope)
    *parts_one, k1v, k2v, g1v, g2v = lower(geo, recv, low, k1, k2, gain_one, gain_two)
    kernels = k1v, k2v, g1v, g2v
    if geo["pairs"]:
        keep2, send2 = parts_two
        mine2, half2 = halve(keep2, swap(send2, "da"))
        keep1, far1, send1, away1 = parts_one
        back = exchange(out)
        away1, half2 = lax.optimization_barrier((swap(away1, "de"), half2))
        far1, send1 = lax.optimization_barrier((fold(far1, away1), send1))
        mine1 = add(keep1, swap(far1, "da"))
        grad_one, grad_two = pull_rows(
            *kernels, mine1, swap(send1, "de"), mine2, swap(half2, "de"))
    else:
        back = exchange(out)
        flat = jnp.stack([x[0].reshape(geo["slots"] * group, fan) for x in (parts_one, parts_two)])
        sums = lax.psum_scatter(flat, ("da", "de"), scatter_dimension=1, tiled=True)
        grad_one, grad_two = pull_rows(*kernels, sums[0], sums[1])
    outputs, input_grad = merge(geo, f, c, back)
    return (
        outputs.reshape(features.shape),
        input_grad.reshape(features.shape),
        grad_one.reshape(kernel_one.shape),
        grad_two.reshape(kernel_two.shape),
    )


def solution(mesh):
    names = ("da", "db", "de", "row", "col")
    nr, nc, dp = mesh.shape["row"], mesh.shape["col"], mesh.shape["dp"]

    def run(features, cotangent, kernel_one, kernel_two, gain_one, gain_two):
        group = kernel_one.shape[2] // 9
        per_block = kernel_one.shape[1] // group
        na = 2 if per_block % 2 == 0 else 1
        nb = per_block // na
        fine = Mesh(mesh.devices.reshape(na, nb, dp // per_block, nr, nc), names)
        dps = ("da", "db", "de")
        cells = P(dps, "row", "col", None)
        rows = P(("row", "col"), dps, None)
        gains = P(("row", "col"), dps)
        return jax.shard_map(
            functools.partial(local, group),
            mesh=fine,
            in_specs=(cells, cells, rows, rows, gains, gains),
            out_specs=(cells, cells, rows, rows),
            check_vma=False,
        )(features, cotangent, kernel_one, kernel_two, gain_one, gain_two)

    return run
```

```python
import functools
import math

import jax
import jax.numpy as jnp
from jax import lax
from jax.experimental import pallas as pl
from jax.experimental.pallas import tpu as pltpu
from jax.sharding import Mesh, PartitionSpec as P

GAMMA = 1.7015043497085571
ALPHA = 0.2
EPS = 1e-06
ROOT = math.sqrt(2.0 / math.pi)
CUBE = 0.044715
F32 = jnp.float32
BF16 = jnp.bfloat16
VMEM_LIMIT = 24 * 1024 * 1024
SMALL = 1
RELAY = 20_000_000_000
FIRST = 3_000_000_000
LOWER = RELAY
SECOND = RELAY
FOLD = 1
HALVE = 1
ADD = 500_000_000
PULL = MERGE = SMALL
STRIP = 4


def act_value(x):
    t = jnp.tanh(x * (ROOT + (CUBE * ROOT) * (x * x)))
    return (0.5 * GAMMA) * x * (1.0 + t)


def act_slope(x):
    sq = x * x
    t = jnp.tanh(x * (ROOT + (CUBE * ROOT) * sq))
    return (0.5 * GAMMA) * ((1.0 + t) + x * (1.0 - t * t) * (ROOT + (3.0 * CUBE * ROOT) * sq))


def act_both(x):
    sq = x * x
    t = jnp.tanh(x * (ROOT + (CUBE * ROOT) * sq))
    up = 1.0 + t
    value = (0.5 * GAMMA) * x * up
    bend = x * (1.0 - t * t) * (ROOT + (3.0 * CUBE * ROOT) * sq)
    return value, (0.5 * GAMMA * ALPHA) * (up + bend)


def params(**kw):
    return pltpu.CompilerParams(vmem_limit_bytes=VMEM_LIMIT, **kw)


def pin(x):
    return pltpu.with_memory_space_constraint(x, pltpu.HBM)


def cost(flops):
    return pl.CostEstimate(flops=flops, bytes_accessed=1, transcendentals=0)


def column(gain_ref):
    rows = gain_ref.shape[1]
    first = lax.broadcasted_iota(jnp.int32, (rows, rows), 0)
    second = lax.broadcasted_iota(jnp.int32, (rows, rows), 1)
    spread = jnp.broadcast_to(gain_ref[...], (rows, rows))
    return jnp.sum(jnp.where(first == second, spread, 0.0), axis=1, keepdims=True)


def std_into(k, g, w):
    fan = k.shape[1]
    kern = k[...]
    cent = kern - jnp.mean(kern, axis=1, keepdims=True)
    var = jnp.mean(cent * cent, axis=1, keepdims=True)
    scale = column(g) * lax.rsqrt(var + EPS) * (1.0 / math.sqrt(fan))
    w[...] = (cent * scale).astype(BF16)


def pull_kernel(k1, k2, g1, g2, *refs):
    *sums, out1, out2 = refs
    half = len(sums) // 2
    for k, g, parts, out, factor in (
            (k1, g1, sums[:half], out1, 1.0), (k2, g2, sums[half:], out2, ALPHA)):
        fan = k.shape[1]
        kern = k[...]
        grad = sum(ref[...].astype(F32) for ref in parts)
        cent = kern - jnp.mean(kern, axis=1, keepdims=True)
        var = jnp.mean(cent * cent, axis=1, keepdims=True)
        inv = lax.rsqrt(var + EPS)
        scale = column(g) * inv * (factor / math.sqrt(fan))
        dot = jnp.mean(grad * cent, axis=1, keepdims=True)
        term = scale * (grad - cent * (inv * inv * dot))
        out[...] = term - jnp.mean(term, axis=1, keepdims=True)


def pull_rows(k1, k2, g1, g2, *sums):
    return pl.pallas_call(
        pull_kernel,
        out_shape=[jax.ShapeDtypeStruct(k1.shape, F32)] * 2,
        name="pull_rows",
        compiler_params=params(),
        cost_estimate=cost(PULL),
    )(k1, k2, g1, g2, *sums)


def prep_kernel(geo, k1, k2, g1, g2, f, c, w1, w2, out, *scratch):
    k1_in, k2_in, g1_in, g2_in, f_in, c_in, stage, sems, sent = scratch
    group, blocks = geo["group"], geo["blocks"]
    span = geo["per_block"] * group

    def bring(src, dst):
        move = pltpu.make_async_copy(src, dst, sems.at[len(moves)])
        moves.append(move)
        move.start()
        return move

    moves, cells = [], []
    for n in range(blocks):
        cut = pl.ds(n * span, span)
        cells.append((bring(f.at[:, cut], f_in.at[:, cut]), bring(c.at[:, cut], c_in.at[:, cut])))
        if n == 0:
            rows = [bring(*pair) for pair in ((k1, k1_in), (g1, g1_in), (k2, k2_in), (g2, g2_in))]
    leaves = []
    for block in range(blocks):
        for move in cells[block]:
            move.wait()
        for b in range(geo["nb"]):
            dst = b * blocks + block
            for slot in range(geo["slots"]):
                at = (block * geo["per_block"] + slot * geo["nb"] + b) * group
                stage[dst, 0, slot] = act_value(f_in[:, at : at + group].astype(F32)).astype(BF16)
                stage[dst, 1, slot] = c_in[:, at : at + group]
            leaves.append(pltpu.make_async_copy(stage.at[dst], out.at[dst], sent.at[dst]))
            leaves[-1].start()
        if block == 0:
            for move in rows[:2]:
                move.wait()
            std_into(k1_in, g1_in, w1)
            for move in rows[2:]:
                move.wait()
            std_into(k2_in, g2_in, w2)
    for move in leaves:
        move.wait()


def prep(geo, k1, k2, g1, g2, f, c):
    args = (k1, k2, g1, g2, f, c)
    dims = (geo["peers"], 2, geo["slots"], f.shape[0], geo["group"])
    vmem, hbm = (pl.BlockSpec(memory_space=m) for m in (pltpu.VMEM, pl.ANY))
    return pl.pallas_call(
        functools.partial(prep_kernel, geo),
        in_specs=[hbm] * 6,
        out_specs=[vmem, vmem, hbm],
        out_shape=[jax.ShapeDtypeStruct(k1.shape, BF16)] * 2 + [jax.ShapeDtypeStruct(dims, BF16)],
        scratch_shapes=[pltpu.VMEM(x.shape, x.dtype) for x in args] + [
            pltpu.VMEM(dims, BF16),
            pltpu.SemaphoreType.DMA((4 + 2 * geo["blocks"],)),
            pltpu.SemaphoreType.DMA((geo["peers"],))],
        name="prep",
        compiler_params=params(),
        cost_estimate=cost(SMALL),
    )(*[pin(x) for x in args])


def merge_kernel(geo, f, c, recv, out, grad, out_in, grad_in, sems):
    group, blocks = geo["group"], geo["blocks"]
    span = geo["per_block"] * group
    moves = []
    for block in range(blocks):
        for b in range(geo["nb"]):
            src = b * blocks + block
            for slot in range(geo["slots"]):
                at = (block * geo["per_block"] + slot * geo["nb"] + b) * group
                x = f[:, at : at + group].astype(F32)
                out_in[:, at : at + group] = (x + recv[src, 0, slot].astype(F32)).astype(BF16)
                grad_in[:, at : at + group] = (
                    c[:, at : at + group].astype(F32)
                    + act_slope(x) * recv[src, 1, slot].astype(F32)
                ).astype(BF16)
        cut = pl.ds(block * span, span)
        for n, (src, dst) in enumerate(((out_in, out), (grad_in, grad))):
            moves.append(pltpu.make_async_copy(
                src.at[:, cut], dst.at[:, cut], sems.at[n, block]))
            moves[-1].start()
    for move in moves:
        move.wait()


def merge(geo, f, c, recv):
    shape = jax.ShapeDtypeStruct(f.shape, BF16)
    return pl.pallas_call(
        functools.partial(merge_kernel, geo),
        out_specs=[pl.BlockSpec(memory_space=pl.ANY)] * 2,
        out_shape=(shape, shape),
        scratch_shapes=[pltpu.VMEM(f.shape, BF16)] * 2 + [
            pltpu.SemaphoreType.DMA((2, geo["blocks"]))],
        name="merge",
        compiler_params=params(),
        cost_estimate=cost(MERGE),
    )(f, c, recv)


def runs(geo, number, at, size):
    rows, cols, width = geo["rows"], geo["cols"], geo["width"]
    b, i = number // geo["images"], number % geo["images"]
    for cell in range(at, at + size, cols):
        line, c = cell // width, cell % width // cols
        r, y = line // rows, line % rows
        yield (b * geo["nr"] + r) * geo["nc"] + c, (i * rows + y) * cols


def read_strip(geo, recv, which, slot, number, at, size):
    cols = geo["cols"]
    return jnp.concatenate([
        recv[peer, which, slot, p : p + cols, :] for peer, p in runs(geo, number, at, size)], axis=0)


def write_strip(geo, out, number, at, value):
    cols = geo["cols"]
    for n, (peer, p) in enumerate(runs(geo, number, at, value.shape[0])):
        out[peer, p : p + cols, :] = value[n * cols : (n + 1) * cols, :]


def strips(geo):
    size = STRIP * geo["width"]
    return [(at, size) for at in range(0, geo["area"], size)]


def column_is(geo, shape, place):
    return lax.broadcasted_iota(jnp.int32, shape, 0) % geo["width"] == place


def clear_rim(geo, x2):
    width, group, area = geo["width"], geo["group"], geo["area"]
    zero = jnp.zeros((width, 2 * group), BF16)
    for n in range(geo["maps"]):
        x2[n, 0:width, :] = zero
        x2[n, width + area : 2 * width + area, :] = zero


def fill_strip(geo, x2, number, at, value):
    width, group, size = geo["width"], geo["group"], value.shape[0]
    right = pltpu.roll(value.astype(F32), size - 1, 0)
    right = jnp.where(column_is(geo, right.shape, width - 1), 0.0, right)
    rows = pl.ds(width + at, size)
    x2[number, rows, 0:group] = value.astype(BF16)
    x2[number, rows, group : 2 * group] = right.astype(BF16)


def around(geo, x2, number):
    width, area = geo["width"], geo["area"]
    return jnp.concatenate([x2[number, pl.ds(dy * width, area), :] for dy in range(3)], axis=1)


def join(geo, pair):
    group = geo["group"]
    left = pltpu.roll(pair[:, group:], 1, 0)
    return pair[:, :group] + jnp.where(column_is(geo, left.shape, 0), 0.0, left)


def forward_weights(geo, w, out):
    group = geo["group"]
    for dy in range(3):
        at = dy * 2 * group
        out[0:group, at : at + 2 * group] = w[:, (3 * dy + 1) * group : (3 * dy + 3) * group]
        out[group : 2 * group, at : at + group] = w[:, 3 * dy * group : (3 * dy + 1) * group]
        out[group : 2 * group, at + group : at + 2 * group] = jnp.zeros((group, group), BF16)


def adjoint_weights(geo, w, out):
    group = geo["group"]
    for row in range(3):
        dy, at = 2 - row, row * 2 * group
        out[at : at + group, :] = w[:, (3 * dy + 1) * group : (3 * dy + 3) * group]
        out[at + group : at + 2 * group, 0:group] = w[:, 3 * dy * group : (3 * dy + 1) * group]
        out[at + group : at + 2 * group, group : 2 * group] = jnp.zeros((group, group), BF16)


def conv(geo, x2, number, at, size, weights, turned):
    span, width = 2 * geo["group"], geo["width"]
    total = None
    for dy in range(3):
        rows = x2[number, pl.ds(at + dy * width, size), :]
        if turned:
            part = jnp.dot(
                rows, weights[dy * span : (dy + 1) * span, :], preferred_element_type=F32)
        else:
            part = lax.dot_general(
                rows, weights[:, dy * span : (dy + 1) * span], (((1,), (1,)), ((), ())),
                preferred_element_type=F32)
        total = part if total is None else total + part
    return join(geo, total)


def terms(geo, g2, x2, out):
    width, area, group = geo["width"], geo["area"], geo["group"]
    total = None
    for n in range(geo["maps"]):
        part = lax.dot_general(
            g2[n, pl.ds(width, area), :], around(geo, x2, n), (((0,), (0,)), ((), ())),
            preferred_element_type=F32)
        total = part if total is None else total + part
    for dy in range(3):
        at, to = dy * 2 * group, dy * 3 * group
        out[:, to + group : to + 3 * group] = total[0:group, at : at + 2 * group]
        out[:, to : to + group] = total[group : 2 * group, at : at + group]


def load_weights(geo, slot, refs, w):
    if not geo["pairs"]:
        w[...] = refs[0][slot]
        return
    e = lax.axis_index("de")
    half = w.shape[0] // 2
    mine = lax.axis_index("da") == slot

    def put(here, there):
        w[pl.ds(pl.multiple_of(e * half, half), half), :] = here[...]
        w[pl.ds(pl.multiple_of((1 - e) * half, half), half), :] = there[...]

    if len(refs) == 2:
        refs = [ref.at[n] for n in range(2) for ref in refs]
    pl.when(mine)(lambda: put(refs[0], refs[1]))
    pl.when(jnp.logical_not(mine))(lambda: put(refs[2], refs[3]))


def split_terms(geo, slot, total, refs):
    if not geo["pairs"]:
        refs[0][slot] = total[...]
        return
    keep_near, keep_far, send_near, send_far = refs
    e = lax.axis_index("de")
    half = keep_near.shape[0]
    mine = lax.axis_index("da") == slot

    def put(keep, send):
        keep[...] = total[pl.ds(pl.multiple_of(e * half, half), half), :]
        send[...] = total[pl.ds(pl.multiple_of((1 - e) * half, half), half), :].astype(BF16)

    pl.when(mine)(lambda: put(keep_near, send_near))
    pl.when(jnp.logical_not(mine))(lambda: put(keep_far, send_far))


def split_slots(geo, slot, total, refs):
    if not geo["pairs"]:
        refs[0][slot] = total[...]
        return
    keep, send = refs
    mine = lax.axis_index("da") == slot

    @pl.when(mine)
    def _():
        keep[...] = total[...]

    @pl.when(jnp.logical_not(mine))
    def _():
        send[...] = total[...].astype(BF16)


def term_out(geo):
    if not geo["pairs"]:
        return [jax.ShapeDtypeStruct((geo["slots"], geo["group"], geo["fan"]), F32)]
    shape = (geo["group"] // 2, geo["fan"])
    return [jax.ShapeDtypeStruct(shape, t) for t in (F32, F32, BF16, BF16)]


def slot_out(geo):
    if not geo["pairs"]:
        return term_out(geo)
    return [jax.ShapeDtypeStruct((geo["group"], geo["fan"]), t) for t in (F32, BF16)]


def map_shape(geo):
    return jax.ShapeDtypeStruct((geo["slots"], geo["maps"], geo["area"], geo["group"]), BF16)


def send_shape(geo):
    return jax.ShapeDtypeStruct(
        (geo["peers"], 2, geo["slots"], geo["piece"], geo["group"]), BF16)


def scratch(geo, pairs, total, *weights):
    fan, group, slots = geo["fan"], geo["group"], geo["slots"]
    rows = geo["area"] + 2 * geo["width"]
    shapes = [pltpu.VMEM((slots, geo["maps"], rows, 2 * group), BF16) for _ in range(pairs)]
    shapes += [pltpu.VMEM((slots,) + dims, BF16) for dims in weights]
    return shapes + ([pltpu.VMEM((slots, group, fan), F32)] if total else [])


def weight_shapes(geo):
    group = geo["group"]
    return (group, geo["fan"]), (2 * group, 6 * group), (6 * group, 2 * group)


def conv_flops(geo):
    return 2 * geo["slots"] * geo["maps"] * geo["area"] * geo["group"] * geo["fan"]


def call(geo, body, name, args, out_shape, scratch_shapes, flops):
    return pl.pallas_call(
        functools.partial(body, geo),
        out_shape=out_shape,
        scratch_shapes=scratch_shapes,
        name=name,
        compiler_params=params(),
        cost_estimate=cost(flops),
    )(*args)


def first_kernel(geo, *refs):
    nw = 2 if geo["pairs"] else 1
    recv, h_out, s_out = refs[nw : nw + 3]
    t_out, buffers = refs[nw + 3 : -6], refs[-6:]
    for slot in range(geo["slots"]):
        x2, y2, g2, w, fw, total = [ref.at[slot] for ref in buffers]
        for buffer in (x2, y2, g2):
            clear_rim(geo, buffer)
        load_weights(geo, slot, refs[:nw], w)
        forward_weights(geo, w, fw)
        for n in range(geo["maps"]):
            for at, size in strips(geo):
                fill_strip(geo, x2, n, at, read_strip(geo, recv, 0, slot, n, at, size))
        for n in range(geo["maps"]):
            for at, size in strips(geo):
                z = conv(geo, x2, n, at, size, fw, False).astype(BF16).astype(F32)
                h, slope = act_both(z)
                h = h.astype(BF16)
                h_out[slot, n, at : at + size, :] = h
                s_out[slot, n, at : at + size, :] = slope.astype(BF16)
                fill_strip(geo, y2, n, at, h)
                fill_strip(geo, g2, n, at, read_strip(geo, recv, 1, slot, n, at, size))
        terms(geo, g2, y2, total)
        split_slots(geo, slot, total, t_out)


def first(geo, one, recv):
    return call(
        geo, first_kernel, "first", (*one, recv),
        [map_shape(geo)] * 2 + slot_out(geo),
        scratch(geo, 3, True, *weight_shapes(geo)[:2]), FIRST)


def second_kernel(geo, nw, *refs):
    one, two = refs[: nw[0]], refs[nw[0] : sum(nw)]
    recv, h_in, s_in, l_out, out, *buffers, low_in, stage, sems, low_sems = refs[sum(nw) :]
    moves = []

    def leave(which, slot):
        move = pltpu.make_async_copy(
            stage.at[which, slot], out.at[:, which, slot], sems.at[which, slot])
        move.start()
        moves.append(move)

    for slot in range(geo["slots"]):
        x2, y2, z2, w, fw2, aw2, aw1 = [ref.at[slot] for ref in buffers]
        for buffer in (x2, y2, z2):
            clear_rim(geo, buffer)
        load_weights(geo, slot, two, w)
        forward_weights(geo, w, fw2)
        adjoint_weights(geo, w, aw2)
        load_weights(geo, slot, one, w)
        adjoint_weights(geo, w, aw1)
        for n in range(geo["maps"]):
            for at, size in strips(geo):
                fill_strip(geo, x2, n, at, h_in[slot, n, at : at + size, :])
        for n in range(geo["maps"]):
            for at, size in strips(geo):
                value = ALPHA * conv(geo, x2, n, at, size, fw2, False)
                write_strip(geo, stage.at[0, slot], n, at, value.astype(BF16))
                fill_strip(geo, y2, n, at, read_strip(geo, recv, 1, slot, n, at, size))
        leave(0, slot)
        for n in range(geo["maps"]):
            for at, size in strips(geo):
                low = conv(geo, y2, n, at, size, aw2, True)
                low = (low * s_in[slot, n, at : at + size, :].astype(F32)).astype(BF16)
                low_in[slot, n, at : at + size, :] = low
                fill_strip(geo, z2, n, at, low)
        moves.append(pltpu.make_async_copy(low_in.at[slot], l_out.at[slot], low_sems.at[slot]))
        moves[-1].start()
        for n in range(geo["maps"]):
            for at, size in strips(geo):
                value = conv(geo, z2, n, at, size, aw1, True)
                write_strip(geo, stage.at[1, slot], n, at, value.astype(BF16))
        leave(1, slot)
    for move in moves:
        move.wait()


def second(geo, one, two, recv, hidden, slope):
    nw = (len(one), len(two))
    shapes = weight_shapes(geo)
    sent = send_shape(geo)
    args = (*one, *two, recv, hidden, slope)
    return pl.pallas_call(
        functools.partial(second_kernel, geo, nw),
        out_shape=[pltpu.HBM(map_shape(geo).shape, BF16), sent],
        out_specs=[pl.BlockSpec(memory_space=pl.ANY)] * 2,
        scratch_shapes=scratch(geo, 3, False, *shapes, shapes[2]) + [
            pltpu.VMEM(map_shape(geo).shape, BF16),
            pltpu.VMEM((2, geo["slots"], geo["peers"], geo["piece"], geo["group"]), BF16),
            pltpu.SemaphoreType.DMA((2, geo["slots"])),
            pltpu.SemaphoreType.DMA((geo["slots"],))],
        name="second",
        compiler_params=params(),
        cost_estimate=cost(SECOND),
    )(*args)


def lower_kernel(geo, recv, low, k1, k2, g1, g2, *refs):
    t_out, (*buffers, l_in, sems, k_sems) = refs[:-6], refs[-6:]
    t_out, held = t_out[:-4], t_out[-4:]
    brought = [pltpu.make_async_copy(src, dst, k_sems.at[n])
               for n, (src, dst) in enumerate(zip((k1, k2, g1, g2), held))]
    slots = range(geo["slots"])
    moves = [pltpu.make_async_copy(low.at[slot], l_in.at[slot], sems.at[slot]) for slot in slots]
    for move in moves:
        move.start()
    for slot in slots:
        x2 = buffers[0].at[slot]
        clear_rim(geo, x2)
        for n in range(geo["maps"]):
            for at, size in strips(geo):
                fill_strip(geo, x2, n, at, read_strip(geo, recv, 0, slot, n, at, size))
    for slot in slots:
        x2, g2, total = [ref.at[slot] for ref in buffers]
        moves[slot].wait()
        if slot == 0:
            for move in brought:
                move.start()
        for n in range(geo["maps"]):
            for at, size in strips(geo):
                fill_strip(geo, g2, n, at, l_in[slot, n, at : at + size, :])
        terms(geo, g2, x2, total)
        split_terms(geo, slot, total, t_out)
    for move in brought:
        move.wait()


def lower(geo, recv, low, *kernels):
    vmem, hbm = (pl.BlockSpec(memory_space=m) for m in (pltpu.VMEM, pl.ANY))
    return pl.pallas_call(
        functools.partial(lower_kernel, geo),
        in_specs=[vmem] + [hbm] * 5,
        out_shape=term_out(geo) + [jax.ShapeDtypeStruct(x.shape, F32) for x in kernels],
        scratch_shapes=scratch(geo, 2, True) + [
            pltpu.VMEM(map_shape(geo).shape, BF16), pltpu.SemaphoreType.DMA((geo["slots"],)),
            pltpu.SemaphoreType.DMA((4,))],
        name="lower",
        compiler_params=params(),
        cost_estimate=cost(LOWER),
    )(recv, pin(low), *[pin(x) for x in kernels])


def fold_kernel(keep, recv, send):
    send[...] = (keep[...] + recv[...].astype(F32)).astype(BF16)


def fold(keep, recv):
    return pl.pallas_call(
        fold_kernel,
        out_shape=jax.ShapeDtypeStruct(keep.shape, BF16),
        name="fold",
        compiler_params=params(),
        cost_estimate=cost(FOLD),
    )(keep, recv)


def halve_kernel(keep, recv, mine, send):
    e = lax.axis_index("de")
    half = mine.shape[0]
    here = pl.ds(pl.multiple_of(e * half, half), half)
    there = pl.ds(pl.multiple_of((1 - e) * half, half), half)
    mine[...] = keep[here, :] + recv[here, :].astype(F32)
    send[...] = (keep[there, :] + recv[there, :].astype(F32)).astype(BF16)


def halve(keep, recv):
    shape = (keep.shape[0] // 2, keep.shape[1])
    return pl.pallas_call(
        halve_kernel,
        out_shape=[jax.ShapeDtypeStruct(shape, F32), jax.ShapeDtypeStruct(shape, BF16)],
        name="halve",
        compiler_params=params(),
        cost_estimate=cost(HALVE),
    )(keep, recv)


def add_kernel(keep, recv, out):
    out[...] = keep[...] + recv[...].astype(F32)


def add(keep, recv):
    return pl.pallas_call(
        add_kernel,
        out_shape=jax.ShapeDtypeStruct(keep.shape, F32),
        name="add",
        compiler_params=params(),
        cost_estimate=cost(ADD),
    )(keep, recv)


def swap(value, axis):
    return lax.ppermute(value, axis, [(0, 1), (1, 0)])


def relay_kernel(rows, over, out):
    out[0] = rows[...]
    out[1] = over[...]


def relay(rows, over):
    return pl.pallas_call(
        relay_kernel,
        out_shape=jax.ShapeDtypeStruct((2,) + rows.shape, rows.dtype),
        name="relay",
        compiler_params=params(),
        cost_estimate=cost(RELAY),
    )(rows, over)


def gather_rows(geo, one, two):
    if not geo["pairs"]:
        full = [lax.all_gather(w, ("da", "de"), axis=0, tiled=True) for w in (one, two)]
        return [(w.reshape(geo["slots"], geo["group"], geo["fan"]),) for w in full]
    over = swap(one, "da")
    two, over = lax.optimization_barrier((two, over))
    one = relay(one, over)
    near, over = swap(two, "de"), swap(two, "da")
    return (one, swap(one, "de")), (two, near, over, swap(over, "de"))


def local(group, features, cotangent, kernel_one, kernel_two, gain_one, gain_two):
    images, rows, cols, chans = features.shape
    fan = kernel_one.shape[2]
    nr, nc = lax.axis_size("row"), lax.axis_size("col")
    na, nb, ne = lax.axis_size("da"), lax.axis_size("db"), lax.axis_size("de")
    blocks = nr * nc
    geo = dict(
        group=group, fan=fan, nr=nr, nc=nc, nb=nb, blocks=blocks, slots=na,
        per_block=chans // blocks // group, peers=nb * blocks, images=images,
        rows=rows, cols=cols, piece=images * rows * cols, width=nc * cols,
        area=nr * rows * nc * cols, maps=nb * images, pairs=na == 2 and ne == 2,
    )
    flat = (images * rows * cols, chans)
    f, c = features.reshape(flat), cotangent.reshape(flat)
    k1, k2 = kernel_one.reshape(-1, fan), kernel_two.reshape(-1, fan)
    w1, w2, pieces = prep(geo, k1, k2, gain_one, gain_two, f, c)

    def exchange(x):
        return lax.all_to_all(x, ("db", "row", "col"), 0, 0, tiled=True)

    recv = exchange(pieces)
    one, two = gather_rows(geo, w1, w2)
    hidden, slope, *parts_two = first(geo, one, recv)
    low, out = second(geo, one, two, recv, hidden, slope)
    *parts_one, k1v, k2v, g1v, g2v = lower(geo, recv, low, k1, k2, gain_one, gain_two)
    kernels = k1v, k2v, g1v, g2v
    if geo["pairs"]:
        keep2, send2 = parts_two
        mine2, half2 = halve(keep2, swap(send2, "da"))
        keep1, far1, send1, away1 = parts_one
        back = exchange(out)
        away1, half2 = lax.optimization_barrier((swap(away1, "de"), half2))
        far1, send1 = lax.optimization_barrier((fold(far1, away1), send1))
        mine1 = add(keep1, swap(far1, "da"))
        grad_one, grad_two = pull_rows(
            *kernels, mine1, swap(send1, "de"), mine2, swap(half2, "de"))
    else:
        back = exchange(out)
        flat = jnp.stack([x[0].reshape(geo["slots"] * group, fan) for x in (parts_one, parts_two)])
        sums = lax.psum_scatter(flat, ("da", "de"), scatter_dimension=1, tiled=True)
        grad_one, grad_two = pull_rows(*kernels, sums[0], sums[1])
    outputs, input_grad = merge(geo, f, c, back)
    return (
        outputs.reshape(features.shape),
        input_grad.reshape(features.shape),
        grad_one.reshape(kernel_one.shape),
        grad_two.reshape(kernel_two.shape),
    )


def solution(mesh):
    names = ("da", "db", "de", "row", "col")
    nr, nc, dp = mesh.shape["row"], mesh.shape["col"], mesh.shape["dp"]

    def run(features, cotangent, kernel_one, kernel_two, gain_one, gain_two):
        group = kernel_one.shape[2] // 9
        per_block = kernel_one.shape[1] // group
        na = 2 if per_block % 2 == 0 else 1
        nb = per_block // na
        fine = Mesh(mesh.devices.reshape(na, nb, dp // per_block, nr, nc), names)
        dps = ("da", "db", "de")
        cells = P(dps, "row", "col", None)
        rows = P(("row", "col"), dps, None)
        gains = P(("row", "col"), dps)
        return jax.shard_map(
            functools.partial(local, group),
            mesh=fine,
            in_specs=(cells, cells, rows, rows, gains, gains),
            out_specs=(cells, cells, rows, rows),
            check_vma=False,
        )(features, cotangent, kernel_one, kernel_two, gain_one, gain_two)

    return run
```
